32 devices in a mesh: dp: 4 (over y, x), mp: 8 (over z, core).
Axes of the slice: x: 2, y: 2, z: 4, core: 2. Of those that a mesh axis runs over, the one named last changes fastest.
Arguments:
- tokens: bfloat16 [1536, 12288], P(('dp', 'mp')), may hold values from -6 to 6
- up_blocks: int32 [192, 3], replicated, may hold values from 0 to 47, as said below
- down_blocks: int32 [192, 3], replicated, may hold values from 0 to 47, as said below
- down_live: int32 [192], replicated, may hold values from 1 to 3, as said below
- up_weight: bfloat16 [192, 3, 256, 256], P('mp'), may hold values from -0.21875 to 0.21875
- low_in: bfloat16 [12288, 256], P('mp'), may hold values from -0.0546875 to 0.0546875
- low_out: bfloat16 [256, 49152], P(None, 'mp'), may hold values from -0.375 to 0.375
- down_weight: bfloat16 [192, 3, 256, 256], P('mp'), may hold values from -0.109375 to 0.109375
- cotangent: bfloat16 [1536, 12288], P(('dp', 'mp')), may hold values from -6 to 6
Outputs:
- mixed: bfloat16 [1536, 12288], P(('dp', 'mp'))
- input_grad: bfloat16 [1536, 12288], P(('dp', 'mp'))
- up_grad: float32 [192, 3, 256, 256], P('mp', None, 'dp')
- down_grad: float32 [192, 3, 256, 256], P('mp', None, 'dp')
- low_out_grad: float32 [256, 49152], P('dp', 'mp')
- low_in_grad: float32 [12288, 256], P('mp', 'dp')
The draws below stay inside these ranges and needn't reach their ends.
Inputs may be any that keep to these rules, and one draw needn't show every extreme that they name: `up_blocks`: row i lists 3 different blocks: first i // 4, then blocks whose index differs from that one in exactly one bit. `down_blocks`: row i lists 3 different blocks: first i // 4, then blocks whose index differs from that one in exactly one bit. `down_live`: some hidden block uses all 3 slots.
All inputs are finite; a program needn't handle non-finite values.
Results may differ from the reference program's by a relative error of at most 0.0075.
Values may be sent and summed in bfloat16 or wider, within the bound.
No kernel may reach another device: no remote copies, remote signals or barrier semaphores. Data moves between devices by JAX's collectives and lax.ppermute only.
A program may use at most 256 MiB of HBM per device.

```python
import jax
import jax.numpy as jnp
from jax import lax

BLK = 256
D = 12288
H = 49152
R = 256
KU = 3
KD = 3
TOKENS = 1536


def butterfly_lists(key, slot_count):
    hidden_count = H // BLK
    width_blocks = D // BLK
    group_size = hidden_count // width_blocks
    home_block = jnp.arange(hidden_count, dtype=jnp.int32) // group_size
    level_count = max(1, (width_blocks - 1).bit_length())
    levels = jnp.arange(level_count, dtype=jnp.int32)
    strides = jnp.array([1 << shift_bits for shift_bits in range(level_count)], jnp.int32)
    parity = home_block[:, None] // strides[None, :] % 2
    partner = home_block[:, None] + jnp.where(parity == 0, strides[None, :], -strides[None, :])
    usable = partner < width_blocks
    jitter_draw = jax.random.randint(key, (hidden_count, level_count), 0, 1 << 20)
    scores = jnp.where(usable, jitter_draw * 64 + levels[None, :], -1)
    _, chosen = lax.top_k(scores, slot_count - 1)
    picked = jnp.take_along_axis(partner, chosen, axis=1)
    return jnp.concatenate([home_block[:, None], picked], axis=1).astype(jnp.int32)


def draw_up_blocks(key, part):
    key = jax.random.fold_in(key, 11)
    return butterfly_lists(key, KU)


def draw_down_blocks(key, part):
    key = jax.random.fold_in(key, 23)
    return butterfly_lists(key, KD)


def draw_down_live(key, part):
    key = jax.random.fold_in(key, 37)
    first_key, second_key = jax.random.split(key)
    hidden_count = H // BLK
    live_count = jax.random.randint(first_key, (hidden_count,), 1, KD + 1)
    full_place = jax.random.randint(second_key, (), 0, hidden_count)
    positions = jnp.arange(hidden_count, dtype=jnp.int32)
    return jnp.where(positions == full_place, KD, live_count).astype(jnp.int32)


def shard_levels(own_key, dims, shards, smallest, largest):
    level = 1.0
    for position, blocks in shards:
        steps = jax.random.uniform(jax.random.fold_in(jax.random.fold_in(own_key, 6), position), (blocks,), jnp.float32, smallest / len(shards), largest / len(shards))
        level = level * jnp.repeat(jnp.exp(steps), dims[position] // blocks).reshape((-1,) + (1,) * (len(dims) - 1 - position))
    return level


def normal_values(own_key, extent, deviation, bound, cuts=(), kind=jnp.bfloat16):
    values = jax.random.normal(own_key, extent, jnp.float32) * deviation
    if len(cuts) > 0:
        values = shard_levels(own_key, extent, cuts, -0.22, 0.18) * values
    return jnp.clip(values, min=-bound, max=bound).astype(kind)


def setup_inputs(seed: int = 0) -> dict:
    arg_keys = jax.random.split(jax.random.key(seed), 10)
    tokens = normal_values(arg_keys[0], (TOKENS, D), 1.0, 6.0, ((0, 32),))
    up_blocks = draw_up_blocks(jax.random.fold_in(arg_keys[9], 71), 0)
    down_blocks = draw_down_blocks(jax.random.fold_in(arg_keys[9], 71), 0)
    down_live = draw_down_live(jax.random.fold_in(arg_keys[9], 71), 0)
    up_weight = normal_values(arg_keys[4], (H // BLK, KU, BLK, BLK), (KU * BLK) ** -0.5, 0.21875, ((0, 8),))
    low_in = normal_values(arg_keys[5], (D, R), D ** -0.5, 0.0546875, ((0, 8),))
    low_out = normal_values(arg_keys[6], (R, H), R ** -0.5, 0.375, ((1, 8),))
    down_weight = normal_values(arg_keys[7], (H // BLK, KD, BLK, BLK), (H // D * KD * BLK) ** -0.5, 0.109375, ((0, 8),))
    cotangent = normal_values(arg_keys[8], (TOKENS, D), 1.0, 6.0, ((0, 32),))
    return dict(tokens=tokens, up_blocks=up_blocks, down_blocks=down_blocks, down_live=down_live, up_weight=up_weight, low_in=low_in, low_out=low_out, down_weight=down_weight, cotangent=cotangent)


def activation(inputs):
    return jax.nn.gelu(inputs, approximate=True)

def reference(tokens, up_blocks, down_blocks, down_live, up_weight, low_in, low_out, down_weight, cotangent):
    tok_total = tokens.shape[0]
    width_size = tokens.shape[1]
    block_size = BLK
    width_blocks = width_size // block_size
    hidden_count = H // BLK
    x_blocks = tokens.reshape(tok_total, width_blocks, block_size).astype(jnp.float32)
    dy_blocks = cotangent.reshape(tok_total, width_blocks, block_size).astype(jnp.float32)
    low_half = jnp.dot(tokens, low_in, preferred_element_type=jnp.float32).astype(jnp.bfloat16)
    low_wide = low_half.astype(jnp.float32)
    slot_ids = jnp.arange(KD, dtype=jnp.int32)

    def forward_pieces(block_index):
        sparse = jnp.einsum('tkb,kbc->tc', jnp.take(x_blocks, up_blocks[block_index], axis=1), up_weight[block_index].astype(jnp.float32))
        column_part = lax.dynamic_slice_in_dim(low_out, block_index * block_size, block_size, 1)
        lifted = jnp.dot(low_half, column_part, preferred_element_type=jnp.float32)
        keep_mask = (slot_ids < down_live[block_index]).astype(jnp.float32)
        masked = down_weight[block_index].astype(jnp.float32) * keep_mask[:, None, None]
        return (sparse + lifted, masked, keep_mask, column_part)

    def forward_step(summed, block_index):
        before, masked, keep_mask, column_part = forward_pieces(block_index)
        hidden = activation(before).astype(jnp.bfloat16)
        pieces = jnp.einsum('tb,kbc->tkc', hidden.astype(jnp.float32), masked).astype(jnp.bfloat16)
        summed = summed.at[:, down_blocks[block_index]].add(pieces.astype(jnp.float32))
        return (summed, None)
    block_ids = jnp.arange(hidden_count, dtype=jnp.int32)
    mixed_sum, _ = lax.scan(forward_step, jnp.zeros((tok_total, width_blocks, block_size), jnp.float32), block_ids)
    mixed = mixed_sum.reshape(tok_total, width_size).astype(jnp.bfloat16)

    def backward_step(running, block_index):
        spread_sum, low_sum = running
        before, masked, keep_mask, column_part = forward_pieces(block_index)
        hidden = activation(before).astype(jnp.bfloat16)
        wanted = jnp.take(dy_blocks, down_blocks[block_index], axis=1)
        back_hidden = jnp.einsum('tkc,kbc->tb', wanted, masked)
        _, pullback = jax.vjp(activation, before)
        back_half = pullback(back_hidden)[0].astype(jnp.bfloat16)
        back_wide = back_half.astype(jnp.float32)
        down_part = jnp.einsum('tb,tkc->kbc', hidden.astype(jnp.float32), wanted) * keep_mask[:, None, None]
        up_part = jnp.einsum('tkb,tc->kbc', jnp.take(x_blocks, up_blocks[block_index], axis=1), back_wide)
        low_cols = jnp.dot(low_wide.T, back_wide)
        low_sum = low_sum + jnp.dot(back_wide, column_part.astype(jnp.float32).T)
        spread = jnp.einsum('tc,kbc->tkb', back_wide, up_weight[block_index].astype(jnp.float32)).astype(jnp.bfloat16)
        spread_sum = spread_sum.at[:, up_blocks[block_index]].add(spread.astype(jnp.float32))
        return ((spread_sum, low_sum), (up_part, down_part, low_cols))
    start_state = (jnp.zeros((tok_total, width_blocks, block_size), jnp.float32), jnp.zeros((tok_total, R), jnp.float32))
    (spread_sum, low_sum), (up_grad, down_grad, low_cols) = lax.scan(backward_step, start_state, block_ids)
    low_out_grad = jnp.transpose(low_cols, (1, 0, 2)).reshape(R, H)
    back_low = low_sum.astype(jnp.bfloat16)
    low_in_grad = jnp.dot(tokens.T, back_low, preferred_element_type=jnp.float32)
    low_side = jnp.dot(back_low, low_in.T, preferred_element_type=jnp.float32).astype(jnp.bfloat16)
    input_grad = (spread_sum.reshape(tok_total, width_size) + low_side.astype(jnp.float32)).astype(jnp.bfloat16)
    return (mixed, input_grad, up_grad, down_grad, low_out_grad, low_in_grad)
```

```python
import functools

import jax
import jax.numpy as jnp
from jax import lax
from jax.experimental import pallas as pl
from jax.experimental.pallas import tpu as pltpu
from jax.sharding import PartitionSpec as P

F32 = jnp.float32
BF16 = jnp.bfloat16
GELU_SCALE = 0.7978845608028654
GELU_CUBE = 0.044715
VMEM_LIMIT = 60 * 1024 * 1024


def dot_nn(a, b):
    return lax.dot_general(a, b, (((1,), (0,)), ((), ())), preferred_element_type=F32)


def dot_nt(a, b):
    return lax.dot_general(a, b, (((1,), (1,)), ((), ())), preferred_element_type=F32)


def dot_tn(a, b):
    return lax.dot_general(a, b, (((0,), (0,)), ((), ())), preferred_element_type=F32)


def column_block(index, size):
    return pl.ds(pl.multiple_of(index * size, size), size)


def copies_in(chunks, positions, held, sems):
    rows = chunks[0].shape[0]
    copies = []
    for number, chunk in enumerate(chunks):
        first = pl.multiple_of(positions[number] * rows, 16)
        copies.append(
            pltpu.make_async_copy(chunk, held.at[pl.ds(first, rows), :], sems.at[number])
        )
    return copies


def fill_zero(total, size):
    @pl.loop(0, total.shape[1] // size)
    def _(block):
        total[:, column_block(block, size)] = jnp.zeros((total.shape[0], size), total.dtype)


def write_out(total, held, outs, out_rows, sems, size):
    @pl.loop(0, total.shape[1] // size)
    def _(block):
        columns = column_block(block, size)
        held[:, columns] = total[:, columns].astype(held.dtype)

    copies = []
    for out in outs:
        for part in range(out.shape[0]):
            number = len(copies)
            first = pl.multiple_of(out_rows[number] * out.shape[1], 16)
            copies.append(
                pltpu.make_async_copy(
                    held.at[pl.ds(first, out.shape[1]), :], out.at[part], sems.at[number]
                )
            )
    for copy in copies:
        copy.start()
    for copy in copies:
        copy.wait()


def forward_kernel(chunk_count, out_count, size, up_ref, down_ref, live_ref, pos_ref, out_ref, *refs):
    chunks = refs[:chunk_count]
    low_half, up_weight, low_out, down_weight, hidden, slope = refs[chunk_count : chunk_count + 6]
    outs = refs[chunk_count + 6 : chunk_count + 6 + out_count]
    held, total, in_sems, out_sems = refs[chunk_count + 6 + out_count :]
    step = pl.program_id(0)
    up_slots = up_weight.shape[1]
    down_slots = down_weight.shape[1]

    @pl.when(step == 0)
    def _():
        copies = copies_in(chunks, pos_ref, held, in_sems)
        for copy in copies:
            copy.start()
        fill_zero(total, size)
        for copy in copies:
            copy.wait()

    before = dot_nn(low_half[...], low_out[...])
    for slot in range(up_slots):
        columns = column_block(up_ref[step * up_slots + slot], size)
        before = before + dot_nn(held[:, columns], up_weight[0, slot])
    square = before * before
    bent = jnp.tanh(GELU_SCALE * before * (1.0 + GELU_CUBE * square))
    half = 0.5 * (1.0 + bent)
    active = (before * half).astype(BF16)
    hidden[0] = active
    slope[0] = half + 0.5 * before * (1.0 - bent * bent) * (
        GELU_SCALE * (1.0 + 3.0 * GELU_CUBE * square)
    )
    for slot in range(down_slots):
        columns = column_block(down_ref[step * down_slots + slot], size)
        weight = jnp.where(slot < live_ref[step], down_weight[0, slot], jnp.zeros((), BF16))
        total[:, columns] += dot_nn(active, weight)

    @pl.when(step == pl.num_programs(0) - 1)
    def _():
        write_out(total, held, outs, out_ref, out_sems, size)


def gradient_kernel(chunk_count, first_step, size, up_ref, down_ref, live_ref, pos_ref, quarter_ref, *refs):
    x_chunks = refs[:chunk_count]
    y_chunks = refs[chunk_count : 2 * chunk_count]
    low_half, hidden, slope, down_weight, low_out = refs[2 * chunk_count : 2 * chunk_count + 5]
    back_half, back_low, up_own, up_send, up_pass, down_own, down_send, down_pass = refs[
        2 * chunk_count + 5 : 2 * chunk_count + 13
    ]
    x_held, y_held, block_grad, x_sems, y_sems = refs[2 * chunk_count + 13 :]
    here = pl.program_id(0)
    step = here + first_step
    up_slots = up_own.shape[1] - 1
    down_slots = down_own.shape[1]
    quarter_rows = up_own.shape[2]

    @pl.when(here == 0)
    def _():
        copies = copies_in(x_chunks, pos_ref, x_held, x_sems)
        copies += copies_in(y_chunks, pos_ref, y_held, y_sems)
        for copy in copies:
            copy.start()
        back_low[...] = jnp.zeros(back_low.shape, F32)
        for copy in copies:
            copy.wait()

    wanted = []
    back_hidden = None
    for slot in range(down_slots):
        columns = column_block(down_ref[step * down_slots + slot], size)
        weight = jnp.where(slot < live_ref[step], down_weight[0, slot], jnp.zeros((), BF16))
        part = dot_nt(y_held[:, columns], weight)
        back_hidden = part if back_hidden is None else back_hidden + part
    back = (back_hidden * slope[0]).astype(BF16)
    back_half[0] = back
    back_low[...] += dot_nt(back, low_out[...])

    def spread_rows(number, own, send, passed, slot, pass_first):
        own[0, slot] = block_grad[number, quarter(0), :]
        passed[0, slot] = block_grad[number, quarter(3 - pass_first), :].astype(BF16)
        send[0, 0, slot] = block_grad[number, quarter(pass_first), :].astype(BF16)
        send[1, 0, slot] = block_grad[number, quarter(3), :].astype(BF16)

    def quarter(which):
        return pl.ds(pl.multiple_of(quarter_ref[which] * quarter_rows, quarter_rows), quarter_rows)

    active = hidden[0]
    for slot in range(down_slots):
        columns = column_block(down_ref[step * down_slots + slot], size)
        keep = (slot < live_ref[step]).astype(F32)
        block_grad[slot] = dot_tn(active, y_held[:, columns]) * keep
    for slot in range(down_slots):
        spread_rows(slot, down_own, down_send, down_pass, slot, 2)
    for slot in range(up_slots):
        columns = column_block(up_ref[step * up_slots + slot], size)
        block_grad[down_slots + slot] = dot_tn(x_held[:, columns], back)
    block_grad[down_slots + up_slots] = dot_tn(low_half[...], back)
    for slot in range(up_slots + 1):
        spread_rows(down_slots + slot, up_own, up_send, up_pass, slot, 1)


def spread_kernel(out_count, size, up_ref, rank_ref, out_ref, *refs):
    back_half, up_weight, back_low, low_in = refs[:4]
    outs = refs[4 : 4 + out_count]
    held, total, out_sems = refs[4 + out_count :]
    step = pl.program_id(0)
    up_slots = up_weight.shape[1]

    @pl.when(step == 0)
    def _():
        fill_zero(total, size)
        first = rank_ref[0] * (low_in.shape[0] // size)

        @pl.loop(0, low_in.shape[0] // size)
        def _(block):
            rows = pl.ds(pl.multiple_of(block * size, size), size)
            side = dot_nt(back_low[...], low_in[rows, :])
            total[:, column_block(first + block, size)] = side

    for slot in range(up_slots):
        columns = column_block(up_ref[step * up_slots + slot], size)
        total[:, columns] += dot_nt(back_half[0], up_weight[0, slot])

    @pl.when(step == pl.num_programs(0) - 1)
    def _():
        write_out(total, held, outs, out_ref, out_sems, size)


def whole_spec(array):
    zeros = (0,) * array.ndim
    return pl.BlockSpec(array.shape, lambda i, *_: zeros)


def any_spec():
    return pl.BlockSpec(memory_space=pl.ANY)


def block_spec(array, first=0):
    rest = (0,) * (array.ndim - 1)
    return pl.BlockSpec((1,) + array.shape[1:], lambda i, *_: (i + first,) + rest)


def params():
    return pltpu.CompilerParams(
        dimension_semantics=("arbitrary",), vmem_limit_bytes=VMEM_LIMIT
    )


def shape(dims, dtype):
    return jax.ShapeDtypeStruct(dims, dtype)


def run_forward(scalars, chunks, low_half, up_weight, low_out, down_weight, out_shapes, size):
    count, tok_total, width = up_weight.shape[0], low_half.shape[0], chunks[0].shape[1]
    out_total = sum(dims[0] for dims in out_shapes)
    hidden = shape((count, tok_total, size), BF16)
    slope = shape((count, tok_total, size), F32)
    products = 2 * up_weight.shape[1] + 1
    return pl.pallas_call(
        functools.partial(forward_kernel, len(chunks), len(out_shapes), size),
        out_shape=[hidden, slope] + [shape(dims, BF16) for dims in out_shapes],
        grid_spec=pltpu.PrefetchScalarGridSpec(
            num_scalar_prefetch=len(scalars),
            grid=(count,),
            in_specs=[any_spec()] * len(chunks)
            + [
                whole_spec(low_half),
                block_spec(up_weight),
                pl.BlockSpec((low_out.shape[0], size), lambda i, *_: (0, i)),
                block_spec(down_weight),
            ],
            out_specs=[block_spec(hidden), block_spec(slope)] + [any_spec()] * len(out_shapes),
            scratch_shapes=[
                pltpu.VMEM((tok_total, width), BF16),
                pltpu.VMEM((tok_total, width), F32),
                pltpu.SemaphoreType.DMA((len(chunks),)),
                pltpu.SemaphoreType.DMA((out_total,)),
            ],
        ),
        compiler_params=params(),
        cost_estimate=pl.CostEstimate(
            flops=2 * products * count * tok_total * size * size,
            bytes_accessed=60_000_000,
            transcendentals=count * tok_total * size,
        ),
        name="forward",
    )(*scalars, *chunks, low_half, up_weight, low_out, down_weight)


def run_gradients(
    scalars, x_chunks, y_chunks, low_half, hidden, slope, down_weight, low_out, first, count, parts, size
):
    tok_total, width = low_half.shape[0], x_chunks[0].shape[1]
    down_slots = down_weight.shape[1]
    up_slots = down_slots
    rows = size // parts
    back_half = shape((count, tok_total, size), BF16)
    back_low = shape(low_half.shape, F32)
    outs = [back_half, back_low]
    specs = [block_spec(back_half), whole_spec(back_low)]
    for slots in (up_slots + 1, down_slots):
        own = shape((count, slots, rows, size), F32)
        send = shape((2, count, slots, rows, size), BF16)
        passed = shape((count, slots, rows, size), BF16)
        outs += [own, send, passed]
        specs += [
            block_spec(own),
            pl.BlockSpec((2, 1, slots, rows, size), lambda i, *_: (0, i, 0, 0, 0)),
            block_spec(passed),
        ]
    return pl.pallas_call(
        functools.partial(gradient_kernel, len(x_chunks), first, size),
        out_shape=outs,
        grid_spec=pltpu.PrefetchScalarGridSpec(
            num_scalar_prefetch=len(scalars),
            grid=(count,),
            in_specs=[any_spec()] * (len(x_chunks) + len(y_chunks))
            + [
                whole_spec(low_half),
                block_spec(hidden, first),
                block_spec(slope, first),
                block_spec(down_weight, first),
                pl.BlockSpec((low_out.shape[0], size), lambda i, *_: (0, i + first)),
            ],
            out_specs=specs,
            scratch_shapes=[
                pltpu.VMEM((tok_total, width), BF16),
                pltpu.VMEM((tok_total, width), BF16),
                pltpu.VMEM((down_slots + up_slots + 1, size, size), F32),
                pltpu.SemaphoreType.DMA((len(x_chunks),)),
                pltpu.SemaphoreType.DMA((len(y_chunks),)),
            ],
        ),
        compiler_params=params(),
        cost_estimate=pl.CostEstimate(
            flops=2 * 11 * count * tok_total * size * size,
            bytes_accessed=50_000_000,
            transcendentals=0,
        ),
        name="gradients",
    )(*scalars, *x_chunks, *y_chunks, low_half, hidden, slope, down_weight, low_out)


def run_spread(scalars, back_half, up_weight, back_low, low_in, out_shapes, width, size):
    count, tok_total = back_half.shape[:2]
    out_total = sum(dims[0] for dims in out_shapes)
    return pl.pallas_call(
        functools.partial(spread_kernel, len(out_shapes), size),
        out_shape=[shape(dims, BF16) for dims in out_shapes],
        grid_spec=pltpu.PrefetchScalarGridSpec(
            num_scalar_prefetch=len(scalars),
            grid=(count,),
            in_specs=[
                block_spec(back_half),
                block_spec(up_weight),
                whole_spec(back_low),
                whole_spec(low_in),
            ],
            out_specs=[any_spec()] * len(out_shapes),
            scratch_shapes=[
                pltpu.VMEM((tok_total, width), BF16),
                pltpu.VMEM((tok_total, width), F32),
                pltpu.SemaphoreType.DMA((out_total,)),
            ],
        ),
        compiler_params=params(),
        cost_estimate=pl.CostEstimate(
            flops=2 * 3 * count * tok_total * size * size,
            bytes_accessed=30_000_000,
            transcendentals=0,
        ),
        name="spread",
    )(*scalars, back_half, up_weight, back_low, low_in)


def local(mp_size, dp_size, tokens, up_blocks, down_blocks, down_live, up_weight, low_in, low_out, down_weight, cotangent):
    count, up_slots, size = up_weight.shape[:3]
    down_slots = down_weight.shape[1]
    rows, width = tokens.shape
    tok_total = rows * mp_size
    col_width = low_in.shape[0]
    rank = lax.axis_index("mp")
    part = lax.axis_index("dp")
    chip, core = rank // 2, rank % 2
    chips = mp_size // 2
    by_ring = rows % 16 == 0
    ring = [(i, (i + 2) % mp_size) for i in range(mp_size)]
    swap = [(i, i ^ 1) for i in range(mp_size)]

    up_index = lax.dynamic_slice_in_dim(up_blocks, rank * count, count, 0).reshape(-1)
    down_index = lax.dynamic_slice_in_dim(down_blocks, rank * count, count, 0).reshape(-1)
    live = lax.dynamic_slice_in_dim(down_live, rank * count, count, 0)
    quarters = part ^ jnp.arange(dp_size, dtype=jnp.int32)

    chip_order = (chip - jnp.arange(chips, dtype=jnp.int32)) % chips
    if by_ring:
        positions = jnp.concatenate([chip_order * 2 + core, chip_order * 2 + (1 - core)])
        out_shapes = [(chips, rows, width), (chips, rows, width)]
    else:
        positions = jnp.zeros((1,), jnp.int32)
        out_shapes = [(1, tok_total, width)]

    def gather(block):
        if not by_ring:
            return [lax.all_gather(block, "mp", axis=0, tiled=True)]
        same = [block]
        for _ in range(chips - 1):
            same.append(lax.ppermute(same[-1], "mp", ring))
        return same + [lax.ppermute(piece, "mp", swap) for piece in same]

    def scatter_sum(parts):
        if not by_ring:
            whole = parts[0].reshape(mp_size, rows, width)
            return lax.psum_scatter(whole, "mp", scatter_dimension=0).reshape(rows, width)
        keep, give = parts
        got = lax.ppermute(give, "mp", swap)

        def mine(place):
            return keep[place].astype(F32) + got[place].astype(F32)

        moving = mine(1 % chips).astype(BF16)
        for place in range(2, chips + 1):
            moving = lax.ppermute(moving, "mp", ring)
            moving = (mine(place % chips) + moving.astype(F32)).astype(BF16)
        return moving

    def sum_all(partial):
        low = lax.psum_scatter(partial, "mp", scatter_dimension=0, tiled=True)
        return lax.all_gather(low.astype(BF16), "mp", axis=0, tiled=True)

    x_chunks = gather(tokens)
    y_chunks = gather(cotangent)

    columns = jnp.concatenate(
        [lax.dynamic_slice_in_dim(piece, rank * col_width, col_width, 1) for piece in x_chunks], 0
    )
    if by_ring:
        back_order = jnp.argsort(positions)
        columns = jnp.take(
            columns.reshape(mp_size, rows, col_width), back_order, axis=0, mode="clip"
        ).reshape(tok_total, col_width)
    low_half = sum_all(jnp.dot(columns, low_in, preferred_element_type=F32))

    hidden, slope, *mixed_parts = run_forward(
        (up_index, down_index, live, positions, positions),
        x_chunks, low_half, up_weight, low_out, down_weight, out_shapes, size,
    )
    mixed = scatter_sum(mixed_parts)

    cuts = 2 if count % 2 == 0 else 1
    step_x = [(i, i ^ 1) for i in range(dp_size)]
    step_y = [(i, i ^ 2) for i in range(dp_size)]

    def exchange(own, send, passed, first, second):
        got = lax.ppermute(send, "dp", first)
        onward = (passed.astype(F32) + got[1].astype(F32)).astype(BF16)
        last = lax.ppermute(onward, "dp", second)
        return own + got[0].astype(F32) + last.astype(F32)

    back_parts, low_parts, up_sums, down_sums = [], [], [], []
    for cut in range(cuts):
        back_half, back_low, up_own, up_send, up_pass, down_own, down_send, down_pass = run_gradients(
            (up_index, down_index, live, positions, quarters),
            x_chunks, y_chunks, low_half, hidden, slope, down_weight, low_out,
            cut * (count // cuts), count // cuts, dp_size, size,
        )
        back_parts.append(back_half)
        low_parts.append(back_low)
        up_sums.append(exchange(up_own, up_send, up_pass, step_x, step_y))
        down_sums.append(exchange(down_own, down_send, down_pass, step_y, step_x))
    back_low = sum_all(sum(low_parts))
    low_in_part = lax.dot_general(
        columns, back_low, (((0,), (0,)), ((), ())), preferred_element_type=F32
    )
    low_in_grad = lax.psum_scatter(low_in_part, "dp", scatter_dimension=1, tiled=True)
    input_parts = run_spread(
        (up_index, rank.reshape(1), positions),
        jnp.concatenate(back_parts, 0), up_weight, back_low, low_in, out_shapes, width, size,
    )
    input_grad = scatter_sum(input_parts)
    up_sum = jnp.concatenate(up_sums, 0)
    down_grad = jnp.concatenate(down_sums, 0)
    up_grad = up_sum[:, :up_slots]
    low_out_grad = jnp.transpose(up_sum[:, up_slots], (1, 0, 2)).reshape(size // dp_size, count * size)
    return (mixed, input_grad, up_grad, down_grad, low_out_grad, low_in_grad)


def solution(mesh):
    return jax.shard_map(
        functools.partial(local, mesh.shape["mp"], mesh.shape["dp"]),
        mesh=mesh,
        in_specs=(
            P(("dp", "mp"), None),
            P(),
            P(),
            P(),
            P("mp", None, None, None),
            P("mp", None),
            P(None, "mp"),
            P("mp", None, None, None),
            P(("dp", "mp"), None),
        ),
        out_specs=(
            P(("dp", "mp"), None),
            P(("dp", "mp"), None),
            P("mp", None, "dp", None),
            P("mp", None, "dp", None),
            P("dp", "mp"),
            P("mp", "dp"),
        ),
        check_vma=False,
    )
```

```python
import functools

import jax
import jax.numpy as jnp
from jax import lax
from jax.experimental import pallas as pl
from jax.experimental.pallas import tpu as pltpu
from jax.sharding import PartitionSpec as P

F32 = jnp.float32
BF16 = jnp.bfloat16
GELU_SCALE = 0.7978845608028654
GELU_CUBE = 0.044715
PER_HIDDEN, PER_PIECES, PER_BACK, PER_GRADIENTS, PER_SPREAD = 4, 6, 4, 3, 6
COST = pl.CostEstimate(flops=1, bytes_accessed=1, transcendentals=0)
VMEM_LIMIT = 60 * 1024 * 1024


def dot_nn(a, b):
    return lax.dot_general(a, b, (((1,), (0,)), ((), ())), preferred_element_type=F32)


def dot_nt(a, b):
    return lax.dot_general(a, b, (((1,), (1,)), ((), ())), preferred_element_type=F32)


def dot_tn(a, b):
    return lax.dot_general(a, b, (((0,), (0,)), ((), ())), preferred_element_type=F32)


def column_block(index, size):
    return pl.ds(pl.multiple_of(index * size, size), size)


def copies_in(chunks, held, sems):
    rows, columns = chunks[0].shape
    blocks = held.shape[0] // rows
    return [
        pltpu.make_async_copy(
            chunk,
            held.at[pl.ds(number % blocks * rows, rows), pl.ds(number // blocks * columns, columns)],
            sems.at[number],
        )
        for number, chunk in enumerate(chunks)
    ]


def fill_zero(total, size):
    @pl.loop(0, total.shape[1] // size)
    def _(block):
        total[:, column_block(block, size)] = jnp.zeros((total.shape[0], size), total.dtype)


def write_out(total, held, outs, sems, size):
    @pl.loop(0, total.shape[1] // size)
    def _(block):
        columns = column_block(block, size)
        held[:, columns] = total[:, columns].astype(held.dtype)

    copies = []
    for number, out in enumerate(outs):
        rows = out.shape[0]
        copies.append(
            pltpu.make_async_copy(held.at[pl.ds(number * rows, rows), :], out, sems.at[number])
        )
    for copy in copies:
        copy.start()
    for copy in copies:
        copy.wait()


def hidden_kernel(chunk_count, wait_count, per, size, up_ref, *refs):
    chunks = refs[:chunk_count]
    low_half, up_weight, low_out = refs[chunk_count : chunk_count + 3]
    hidden, slope, held, in_sems = refs[chunk_count + 3 + wait_count :]
    up_slots = up_weight.shape[1]

    @pl.when(pl.program_id(0) == 0)
    def _():
        copies = copies_in(chunks, held, in_sems)
        for copy in copies:
            copy.start()
        for copy in copies:
            copy.wait()

    for inner in range(per):
        first = (pl.program_id(0) * per + inner) * up_slots
        picked = [held[:, column_block(up_ref[first + slot], size)] for slot in range(up_slots)]
        weights = [up_weight[inner, slot] for slot in range(up_slots)]
        before = dot_nn(
            jnp.concatenate(picked + [low_half[...]], axis=1),
            jnp.concatenate(weights + [low_out[:, inner * size : (inner + 1) * size]], axis=0),
        )
        square = before * before
        bent = jnp.tanh(GELU_SCALE * before * (1.0 + GELU_CUBE * square))
        half = 0.5 * (1.0 + bent)
        hidden[inner] = (before * half).astype(BF16)
        slope[inner] = half + 0.5 * before * (1.0 - bent * bent) * (
            GELU_SCALE * (1.0 + 3.0 * GELU_CUBE * square)
        )


def pieces_kernel(out_count, wait_count, per, size, down_ref, live_ref, *refs):
    hidden, down_weight = refs[:2]
    first_out = 2 + wait_count
    outs = refs[first_out : first_out + out_count]
    held, total, out_sems = refs[first_out + out_count :]
    down_slots = down_weight.shape[1]

    @pl.when(pl.program_id(0) == 0)
    def _():
        fill_zero(total, size)

    for inner in range(per):
        step = pl.program_id(0) * per + inner
        weights = [
            jnp.where(slot < live_ref[step], down_weight[inner, slot], jnp.zeros((), BF16))
            for slot in range(down_slots)
        ]
        pieces = dot_nn(hidden[inner], jnp.concatenate(weights, axis=1))
        for slot in range(down_slots):
            columns = column_block(down_ref[step * down_slots + slot], size)
            total[:, columns] += pieces[:, slot * size : (slot + 1) * size]

    @pl.when(pl.program_id(0) == pl.num_programs(0) - 1)
    def _():
        write_out(total, held, outs, out_sems, size)


def back_kernel(chunk_count, wait_count, per, size, down_ref, live_ref, *refs):
    chunks = refs[:chunk_count]
    slope, down_weight, low_out = refs[chunk_count : chunk_count + 3]
    back_half, back_low, held, sems = refs[chunk_count + 3 + wait_count :]
    down_slots = down_weight.shape[1]

    @pl.when(pl.program_id(0) == 0)
    def _():
        copies = copies_in(chunks, held, sems)
        for copy in copies:
            copy.start()
        back_low[...] = jnp.zeros(back_low.shape, F32)
        for copy in copies:
            copy.wait()

    backs = []
    for inner in range(per):
        step = pl.program_id(0) * per + inner
        wanted = [
            held[:, column_block(down_ref[step * down_slots + slot], size)]
            for slot in range(down_slots)
        ]
        weights = [
            jnp.where(slot < live_ref[step], down_weight[inner, slot], jnp.zeros((), BF16))
            for slot in range(down_slots)
        ]
        back_hidden = dot_nt(jnp.concatenate(wanted, axis=1), jnp.concatenate(weights, axis=1))
        back = (back_hidden * slope[inner]).astype(BF16)
        back_half[inner] = back
        backs.append(back)
    back_low[...] += dot_nt(jnp.concatenate(backs, axis=1), low_out[...])


def load_all(chunks, held, sems):
    @pl.when(pl.program_id(0) == 0)
    def _():
        copies = copies_in(chunks, held, sems)
        for copy in copies:
            copy.start()
        for copy in copies:
            copy.wait()


def write_groups(groups, outs, per, make):
    first = 0
    for number, (length, way) in enumerate(groups):
        steps = length // per
        inside = (pl.program_id(0) >= first) & (pl.program_id(0) < first + steps)

        @pl.when(inside)
        def _(number=number, way=way):
            own, send, passed = outs[3 * number : 3 * number + 3]
            for inner in range(per):
                for slot in range(own.shape[1]):
                    own[inner, slot] = make(inner, slot, 0)
                    passed[inner, slot] = make(inner, slot, 3 - way).astype(BF16)
                    send[0, inner, slot] = make(inner, slot, way).astype(BF16)
                    send[1, inner, slot] = make(inner, slot, 3).astype(BF16)

        first += steps


def down_kernel(
    chunk_count, wait_count, first_step, per, groups, size, down_ref, live_ref, quarter_ref, *refs
):
    chunks = refs[:chunk_count]
    hidden = refs[chunk_count]
    outs = refs[chunk_count + 1 + wait_count : -3]
    held, part, sems = refs[-3:]
    slots, rows = outs[0].shape[1:3]
    load_all(chunks, held, sems)
    step = first_step + pl.program_id(0) * per
    for inner in range(per):
        wanted = [
            held[:, column_block(down_ref[(step + inner) * slots + slot], size)]
            for slot in range(slots)
        ]
        part[inner] = dot_tn(hidden[inner], jnp.concatenate(wanted, axis=1))

    def make(inner, slot, which):
        keep = (slot < live_ref[step + inner]).astype(F32)
        first = pl.multiple_of(quarter_ref[which] * rows, rows)
        return part[inner, pl.ds(first, rows), slot * size : (slot + 1) * size] * keep

    write_groups(groups, outs, per, make)


def up_kernel(chunk_count, wait_count, first_step, per, groups, size, up_ref, quarter_ref, *refs):
    chunks = refs[:chunk_count]
    low_half, back_half = refs[chunk_count : chunk_count + 2]
    outs = refs[chunk_count + 2 + wait_count : -3]
    held, part, sems = refs[-3:]
    slots, rows = outs[0].shape[1] - 1, outs[0].shape[2]
    load_all(chunks, held, sems)
    step = first_step + pl.program_id(0) * per
    for inner in range(per):
        picked = [
            held[:, column_block(up_ref[(step + inner) * slots + slot], size)]
            for slot in range(slots)
        ]
        part[inner] = dot_tn(jnp.concatenate(picked + [low_half[...]], axis=1), back_half[inner])

    def make(inner, slot, which):
        first = pl.multiple_of(quarter_ref[which] * rows + slot * size, rows)
        return part[inner, pl.ds(first, rows), :]

    write_groups(groups, outs, per, make)


def spread_kernel(out_count, wait_count, per, size, up_ref, rank_ref, *refs):
    back_half, up_weight, back_low, low_in = refs[:4]
    first_out = 4 + wait_count
    outs = refs[first_out : first_out + out_count]
    held, total, out_sems = refs[first_out + out_count :]
    up_slots = up_weight.shape[1]

    @pl.when(pl.program_id(0) == 0)
    def _():
        fill_zero(total, size)
        first = rank_ref[0] * (low_in.shape[0] // size)

        @pl.loop(0, low_in.shape[0] // size)
        def _(block):
            rows = pl.ds(pl.multiple_of(block * size, size), size)
            side = dot_nt(back_low[...], low_in[rows, :])
            total[:, column_block(first + block, size)] = side

    for inner in range(per):
        step = pl.program_id(0) * per + inner
        weights = jnp.concatenate([up_weight[inner, slot] for slot in range(up_slots)], axis=0)
        spread = dot_nt(back_half[inner], weights)
        for slot in range(up_slots):
            columns = column_block(up_ref[step * up_slots + slot], size)
            total[:, columns] += spread[:, slot * size : (slot + 1) * size]

    @pl.when(pl.program_id(0) == pl.num_programs(0) - 1)
    def _():
        write_out(total, held, outs, out_sems, size)


def whole_spec(array):
    zeros = (0,) * array.ndim
    return pl.BlockSpec(array.shape, lambda i, *_: zeros)


def any_spec():
    return pl.BlockSpec(memory_space=pl.ANY)


def block_spec(array, per, first=0):
    rest = (0,) * (array.ndim - 1)
    return pl.BlockSpec((per,) + array.shape[1:], lambda i, *_: (i + first // per,) + rest)


def blocks_per_step(count, most):
    return max(per for per in range(1, most + 1) if count % per == 0)


def params():
    return pltpu.CompilerParams(
        dimension_semantics=("arbitrary",), vmem_limit_bytes=VMEM_LIMIT
    )


def shape(dims, dtype):
    return jax.ShapeDtypeStruct(dims, dtype)


def run_hidden(scalars, chunks, low_half, up_weight, low_out, waits, size):
    count, tok_total, width = up_weight.shape[0], low_half.shape[0], chunks[0].shape[1]
    per = blocks_per_step(count, PER_HIDDEN)
    hidden = shape((count, tok_total, size), BF16)
    slope = shape((count, tok_total, size), F32)
    return pl.pallas_call(
        functools.partial(hidden_kernel, len(chunks), len(waits), per, size),
        out_shape=[hidden, slope],
        grid_spec=pltpu.PrefetchScalarGridSpec(
            num_scalar_prefetch=len(scalars),
            grid=(count // per,),
            in_specs=[any_spec()] * len(chunks)
            + [
                whole_spec(low_half),
                block_spec(up_weight, per),
                pl.BlockSpec((low_out.shape[0], per * size), lambda i, *_: (0, i)),
            ]
            + [any_spec()] * len(waits),
            out_specs=[block_spec(hidden, per), block_spec(slope, per)],
            scratch_shapes=[
                pltpu.VMEM((tok_total, width), BF16),
                pltpu.SemaphoreType.DMA((len(chunks),)),
            ],
        ),
        compiler_params=params(),
        cost_estimate=COST,
        name="hidden",
    )(*scalars, *chunks, low_half, up_weight, low_out, *waits)


def run_pieces(scalars, hidden, down_weight, waits, out_shapes, width, size):
    count, tok_total = hidden.shape[:2]
    per = blocks_per_step(count, PER_PIECES)
    return pl.pallas_call(
        functools.partial(pieces_kernel, len(out_shapes), len(waits), per, size),
        out_shape=[shape(dims, BF16) for dims in out_shapes],
        grid_spec=pltpu.PrefetchScalarGridSpec(
            num_scalar_prefetch=len(scalars),
            grid=(count // per,),
            in_specs=[block_spec(hidden, per), block_spec(down_weight, per)] + [any_spec()] * len(waits),
            out_specs=[any_spec()] * len(out_shapes),
            scratch_shapes=[
                pltpu.VMEM((tok_total, width), BF16),
                pltpu.VMEM((tok_total, width), F32),
                pltpu.SemaphoreType.DMA((len(out_shapes),)),
            ],
        ),
        compiler_params=params(),
        cost_estimate=COST,
        name="pieces",
    )(*scalars, hidden, down_weight, *waits)


def run_back(scalars, chunks, slope, down_weight, low_out, waits, width, size):
    count, tok_total = slope.shape[:2]
    per = blocks_per_step(count, PER_BACK)
    back_half = shape((count, tok_total, size), BF16)
    back_low = shape((tok_total, low_out.shape[0]), F32)
    return pl.pallas_call(
        functools.partial(back_kernel, len(chunks), len(waits), per, size),
        out_shape=[back_half, back_low],
        grid_spec=pltpu.PrefetchScalarGridSpec(
            num_scalar_prefetch=len(scalars),
            grid=(count // per,),
            in_specs=[any_spec()] * len(chunks)
            + [
                block_spec(slope, per),
                block_spec(down_weight, per),
                pl.BlockSpec((low_out.shape[0], per * size), lambda i, *_: (0, i)),
            ]
            + [any_spec()] * len(waits),
            out_specs=[block_spec(back_half, per), whole_spec(back_low)],
            scratch_shapes=[
                pltpu.VMEM((tok_total, width), BF16),
                pltpu.SemaphoreType.DMA((len(chunks),)),
            ],
        ),
        compiler_params=params(),
        cost_estimate=COST,
        name="back",
    )(*scalars, *chunks, slope, down_weight, low_out, *waits)


def run_gradients(
    kernel, scalars, chunks, whole, blocks, waits, first, groups, slots, part_shape, parts, width
):
    per = min(blocks_per_step(length, PER_GRADIENTS) for length, _ in groups)
    tok_total, size = blocks.shape[1:]
    rows = size // parts
    outs, specs, step = [], [], 0
    for length, _ in groups:
        last = length // per - 1

        def place(i, start=step, last=last):
            return jnp.clip(i - start, 0, last)

        outs += [
            shape((length, slots, rows, size), F32),
            shape((2, length, slots, rows, size), BF16),
            shape((length, slots, rows, size), BF16),
        ]
        one = pl.BlockSpec((per, slots, rows, size), lambda i, *_, at=place: (at(i), 0, 0, 0))
        two = pl.BlockSpec((2, per, slots, rows, size), lambda i, *_, at=place: (0, at(i), 0, 0, 0))
        specs += [one, two, one]
        step += length // per
    results = pl.pallas_call(
        functools.partial(kernel, len(chunks), len(waits), first, per, groups, size),
        out_shape=outs,
        grid_spec=pltpu.PrefetchScalarGridSpec(
            num_scalar_prefetch=len(scalars),
            grid=(step,),
            in_specs=[any_spec()] * len(chunks)
            + [whole_spec(array) for array in whole]
            + [block_spec(blocks, per, first)]
            + [any_spec()] * len(waits),
            out_specs=specs,
            scratch_shapes=[
                pltpu.VMEM((tok_total, width), BF16),
                pltpu.VMEM((per,) + part_shape, F32),
                pltpu.SemaphoreType.DMA((len(chunks),)),
            ],
        ),
        compiler_params=params(),
        cost_estimate=COST,
        name=kernel.__name__,
    )(*scalars, *chunks, *whole, blocks, *waits)
    return [results[3 * number : 3 * number + 3] for number in range(len(groups))]


def run_spread(scalars, back_half, up_weight, back_low, low_in, waits, out_shapes, width, size):
    count, tok_total = back_half.shape[:2]
    per = blocks_per_step(count, PER_SPREAD)
    return pl.pallas_call(
        functools.partial(spread_kernel, len(out_shapes), len(waits), per, size),
        out_shape=[shape(dims, BF16) for dims in out_shapes],
        grid_spec=pltpu.PrefetchScalarGridSpec(
            num_scalar_prefetch=len(scalars),
            grid=(count // per,),
            in_specs=[
                block_spec(back_half, per),
                block_spec(up_weight, per),
                whole_spec(back_low),
                whole_spec(low_in),
            ]
            + [any_spec()] * len(waits),
            out_specs=[any_spec()] * len(out_shapes),
            scratch_shapes=[
                pltpu.VMEM((tok_total, width), BF16),
                pltpu.VMEM((tok_total, width), F32),
                pltpu.SemaphoreType.DMA((len(out_shapes),)),
            ],
        ),
        compiler_params=params(),
        cost_estimate=COST,
        name="spread",
    )(*scalars, back_half, up_weight, back_low, low_in, *waits)


def pass_kernel(half_count, *refs):
    out, first = refs[-1], 0
    for half in range(half_count):
        passed, got = refs[2 * half : 2 * half + 2]
        length = passed.shape[0]
        out[first : first + length] = (passed[...].astype(F32) + got[0].astype(F32)).astype(BF16)
        first += length


def run_pass(halves):
    length = sum(passed.shape[0] for passed, _ in halves)
    out = shape((length,) + halves[0][0].shape[1:], BF16)
    specs = []
    for passed, got in halves:
        specs += [
            whole_spec(passed),
            pl.BlockSpec((1,) + got.shape[1:], lambda i: (1, 0, 0, 0, 0)),
        ]
    return pl.pallas_call(
        functools.partial(pass_kernel, len(halves)),
        out_shape=out,
        grid=(1,),
        in_specs=specs,
        out_specs=whole_spec(out),
        compiler_params=params(),
        cost_estimate=COST,
        name="pass_on",
    )(*[array for pair in halves for array in pair])


def add_kernel(*refs):
    total = refs[0][...].astype(F32)
    for part in refs[1:-1]:
        total = total + part[...].astype(F32)
    refs[-1][...] = total.astype(BF16)


def run_add(arrays):
    rows, width = arrays[0].shape
    steps = 4 if width % 512 == 0 else 1
    spec = pl.BlockSpec((rows, width // steps), lambda i: (0, i))
    return pl.pallas_call(
        add_kernel,
        out_shape=shape((rows, width), BF16),
        grid=(steps,),
        in_specs=[spec] * len(arrays),
        out_specs=spec,
        compiler_params=params(),
        cost_estimate=COST,
        name="add_rows",
    )(*arrays)


def side_kernel(columns, back_low, out):
    out[...] = dot_tn(columns[...], back_low[...]).astype(BF16)


def run_side(columns, back_low, size):
    return pl.pallas_call(
        side_kernel,
        out_shape=shape((columns.shape[1], back_low.shape[1]), BF16),
        grid=(1,),
        in_specs=[whole_spec(columns), whole_spec(back_low)],
        out_specs=pl.BlockSpec((columns.shape[1], back_low.shape[1]), lambda i: (0, 0)),
        compiler_params=params(),
        cost_estimate=COST,
        name="low_in_part",
    )(columns, back_low)


def fence(values, waits):
    values, waits = list(values), list(waits)
    return list(pl.pallas_call(
        lambda *refs: None,
        out_shape=[shape(value.shape, value.dtype) for value in values],
        in_specs=[any_spec()] * (len(values) + len(waits)),
        out_specs=[any_spec()] * len(values),
        input_output_aliases={number: number for number in range(len(values))},
        compiler_params=pltpu.CompilerParams(vmem_limit_bytes=VMEM_LIMIT),
        cost_estimate=COST,
        name="fence",
    )(*values, *waits))


def local(mp_size, dp_size, tokens, up_blocks, down_blocks, down_live, up_weight, low_in, low_out, down_weight, cotangent):
    count, up_slots, size = up_weight.shape[:3]
    rows, width = tokens.shape
    tok_total = rows * mp_size
    col_width = low_in.shape[0]
    rank = lax.axis_index("mp")
    part = lax.axis_index("dp")
    chips = mp_size // 2
    by_ring = rows % 16 == 0 and chips == 4
    swap = [(i, i ^ 1) for i in range(mp_size)]
    step_x = [(i, i ^ 1) for i in range(dp_size)]
    step_y = [(i, i ^ 2) for i in range(dp_size)]

    up_index = lax.dynamic_slice_in_dim(up_blocks, rank * count, count, 0).reshape(-1)
    down_index = lax.dynamic_slice_in_dim(down_blocks, rank * count, count, 0).reshape(-1)
    live = lax.dynamic_slice_in_dim(down_live, rank * count, count, 0)
    quarters = part ^ jnp.arange(dp_size, dtype=jnp.int32)
    out_shapes = [(rows, width)] * mp_size if by_ring else [(tok_total, width)]

    def swapped(piece):
        return lax.ppermute(piece, "mp", swap)

    def shifted(piece, by):
        return lax.ppermute(piece, "mp", [(i, (i + 2 * by) % mp_size) for i in range(mp_size)])

    def add_round(parts, given, place, *moved):
        return run_add([parts[place % chips], given[place % chips], *moved])

    def scatter_whole(parts):
        whole = parts[0].reshape(mp_size, rows, width)
        return lax.psum_scatter(whole, "mp", scatter_dimension=0)

    def over_dp(value, way):
        return lax.ppermute(value, "dp", step_y if way == 2 else step_x)

    def pass_on(parts, gots):
        return [
            run_pass([(part[n][2], got[n]) for part, got in zip(parts, gots)])
            for n in range(len(groups))
        ]

    def sum_rows(chip_sums):
        low = chip_sums[0]
        for back in range(1, chips):
            low = low + shifted(chip_sums[back], -back)
        low = low.astype(BF16)
        same = jnp.concatenate([low] + [shifted(low, back) for back in range(1, chips)], 0)
        return same, jnp.concatenate([same, swapped(same)], 0)

    def sum_whole(partial):
        low = lax.psum_scatter(partial, "mp", scatter_dimension=0, tiled=True).astype(BF16)
        return lax.all_gather(low, "mp", axis=0, tiled=True)

    def take_columns(piece, place):
        return lax.dynamic_slice_in_dim(piece, place * col_width, col_width, 1)

    if by_ring:
        both_low = jnp.concatenate([low_in, swapped(low_in)], 0)
        x_same, chip_sums = [tokens], []
        for step in range(chips):
            both = [take_columns(x_same[step], rank), take_columns(x_same[step], rank ^ 1)]
            chip_sums.append(
                jnp.dot(jnp.concatenate(both, 1), both_low, preferred_element_type=F32)
            )
            if step < chips - 1:
                x_same.append(shifted(x_same[step], 1))
        x_chunks = x_same + [swapped(piece) for piece in x_same]
        low_same, low_half = sum_rows(chip_sums)
        y_same, y_other = [cotangent], [swapped(cotangent)]
        arriving = shifted(fence([cotangent], [low_same])[0], 1)
    else:
        x_chunks = [lax.all_gather(tokens, "mp", axis=0, tiled=True)]
        y_chunks = [lax.all_gather(cotangent, "mp", axis=0, tiled=True)]
        low = jnp.dot(take_columns(x_chunks[0], rank), low_in, preferred_element_type=F32)
        low_half = sum_whole(low)
    columns = jnp.concatenate([take_columns(piece, rank) for piece in x_chunks], 0)
    hidden, slope = run_hidden((up_index,), x_chunks, low_half, up_weight, low_out, [], size)
    if by_ring:
        arrived, hidden = fence([arriving, hidden], y_other + [slope])
        y_same.append(arrived)
        y_other.append(swapped(arrived))
        arriving = shifted(arrived, 1)
    mixed_parts = list(
        run_pieces((down_index, live), hidden, down_weight, [], out_shapes, width, size)
    )
    if by_ring:
        arrived, *mixed_parts[chips:] = fence(
            [arriving] + mixed_parts[chips:], y_other + [columns]
        )
        y_same.append(arrived)
        y_other.append(swapped(arrived))
        arriving = shifted(arrived, 1)
        mixed_given = [None] + [swapped(piece) for piece in mixed_parts[chips + 1 :]]
        arrived = fence([arriving], mixed_given[1:] + y_other)[0]
        y_same.append(arrived)
        y_other.append(swapped(arrived))
        y_chunks = y_same + y_other

    down_slots = down_weight.shape[1]
    if count % 4 == 0:
        groups = ((count // 4, 2), (count // 4, 1))
        starts = (0, count // 2)
    else:
        groups, starts = ((count, 2),), (0,)

    def down_part(start, waits):
        return run_gradients(
            down_kernel, (down_index, live, quarters), y_chunks, [], hidden, waits, start, groups,
            down_slots, (size, down_slots * size), dp_size, width,
        )

    def up_part(start, waits):
        return run_gradients(
            up_kernel, (up_index, quarters), x_chunks, [low_half], back_half, waits, start, groups,
            up_slots + 1, ((up_slots + 1) * size, size), dp_size, width,
        )

    def send_round(parts, moving, waits, give=()):
        here = [part[1] for part in parts]
        sent = fence(here + moving + list(give), waits)
        got = [over_dp(value, way) for value, (_, way) in zip(sent, groups)]
        rest = sent[len(here) :]
        moved = [shifted(value, 1) for value in rest[: len(moving)]]
        return sent[0], got, moved, [swapped(value) for value in rest[len(moving) :]]

    down_parts = [down_part(starts[0], [])]
    moving = [add_round(mixed_parts, mixed_given, 1)] if by_ring else []
    token, got, moving, _ = send_round(down_parts[0], moving, [])
    down_got = [got]
    back_half, back_low = run_back(
        (down_index, live), y_chunks, slope, down_weight, low_out, [token], width, size
    )
    if len(starts) > 1:
        down_parts.append(down_part(starts[1], [back_half]))
    if by_ring:
        moving = [add_round(mixed_parts, mixed_given, 2, moving[0])]
        back_low = fence([back_low], down_got[0] + moving + [down_parts[-1][0][0]])[0]
        half = tok_total // 2
        chip_sum = back_low[:half] + swapped(back_low[half:])
        _, back_low = sum_rows([chip_sum[n * rows : (n + 1) * rows] for n in range(chips)])
    else:
        back_low = sum_whole(back_low)
    if len(starts) > 1:
        give = mixed_parts[chips : chips + 1] if by_ring else []
        token, got, moving, given = send_round(
            down_parts[1], moving, down_got[0] + [back_low], give
        )
        down_got.append(got)

    up_parts, waits = [], [token]
    for start in starts:
        up_parts.append(up_part(start, waits))
        waits = [up_parts[-1][0][0]]
    if by_ring:
        mixed_given[0] = given[0]
        moving = [add_round(mixed_parts, mixed_given, 3, moving[0])]
        waits = waits + given
    token, got, moving, _ = send_round(up_parts[0], moving, down_got[-1] + waits)
    up_got = [got]
    input_parts = list(
        run_spread(
            (up_index, rank.reshape(1)),
            back_half, up_weight, back_low, low_in, [token], out_shapes, width, size,
        )
    )
    low_in_part = run_side(columns, back_low, size)
    down_onward = pass_on(down_parts, down_got)
    waits, give = up_got[0] + down_onward + [low_in_part], []
    if by_ring:
        mixed = add_round(mixed_parts, mixed_given, chips, moving[0])
        waits, give = waits + [mixed], input_parts[chips + 1 : chips + 3]
    else:
        mixed, input_grad = scatter_whole(mixed_parts), scatter_whole(input_parts)
    if len(starts) > 1:
        token, got, _, given = send_round(up_parts[1], [], waits, give)
        up_got.append(got)
    if by_ring:
        input_given = [None] + given
        moving = [shifted(add_round(input_parts, input_given, 1), 1)]
        moving = [add_round(input_parts, input_given, 2, moving[0])]

    def last_round(onward, moving, waits, give=()):
        sent = fence(onward + moving + list(give), waits)
        last = [over_dp(value, 3 - way) for value, (_, way) in zip(sent, groups)]
        rest = sent[len(groups) :]
        moved = [shifted(value, 1) for value in rest[: len(moving)]]
        return last, moved, [swapped(value) for value in rest[len(moving) :]]

    def total(parts, gots, last):
        sums = []
        for half, (part, got) in enumerate(zip(parts, gots)):
            for n, (length, _) in enumerate(groups):
                second = last[n][half * length : (half + 1) * length]
                sums.append(part[n][0] + got[n][0].astype(F32) + second.astype(F32))
        return jnp.concatenate(sums, 0)

    give = [input_parts[chips + 3]] if by_ring else []
    down_last, moving, given = last_round(down_onward, moving, up_got[-1], give)
    if by_ring:
        input_given.append(given[0])
        moving = [add_round(input_parts, input_given, 3, moving[0])]
        give = [input_parts[chips]]
    up_last, moving, given = last_round(pass_on(up_parts, up_got), moving, down_last, give)
    if by_ring:
        input_given[0] = given[0]
        input_grad = add_round(input_parts, input_given, chips, moving[0])

    low_in_grad = lax.psum_scatter(
        low_in_part, "dp", scatter_dimension=1, tiled=True
    ).astype(F32)
    down_grad = total(down_parts, down_got, down_last)
    up_sum = total(up_parts, up_got, up_last)
    up_grad = up_sum[:, :up_slots]
    low_out_grad = jnp.transpose(up_sum[:, up_slots], (1, 0, 2)).reshape(-1, count * size)
    return (mixed, input_grad, up_grad, down_grad, low_out_grad, low_in_grad)


def solution(mesh):
    return jax.shard_map(
        functools.partial(local, mesh.shape["mp"], mesh.shape["dp"]),
        mesh=mesh,
        in_specs=(
            P(("dp", "mp"), None),
            P(),
            P(),
            P(),
            P("mp", None, None, None),
            P("mp", None),
            P(None, "mp"),
            P("mp", None, None, None),
            P(("dp", "mp"), None),
        ),
        out_specs=(
            P(("dp", "mp"), None),
            P(("dp", "mp"), None),
            P("mp", None, "dp", None),
            P("mp", None, "dp", None),
            P("dp", "mp"),
            P("mp", "dp"),
        ),
        check_vma=False,
    )
```

```python
import functools

import jax
import jax.numpy as jnp
from jax import lax
from jax.experimental import pallas as pl
from jax.experimental.pallas import tpu as pltpu
from jax.sharding import PartitionSpec as P

F32 = jnp.float32
BF16 = jnp.bfloat16
GELU_SCALE = 0.7978845608028654
GELU_CUBE = 0.044715
PER_HIDDEN, PER_PIECES, PER_BACK, PER_GRADIENTS, PER_SPREAD = 4, 6, 4, 3, 6
COST = pl.CostEstimate(flops=1, bytes_accessed=1, transcendentals=0)
VMEM_LIMIT = 60 * 1024 * 1024


def dot_nn(a, b):
    return lax.dot_general(a, b, (((1,), (0,)), ((), ())), preferred_element_type=F32)


def dot_nt(a, b):
    return lax.dot_general(a, b, (((1,), (1,)), ((), ())), preferred_element_type=F32)


def dot_tn(a, b):
    return lax.dot_general(a, b, (((0,), (0,)), ((), ())), preferred_element_type=F32)


def column_block(index, size):
    return pl.ds(pl.multiple_of(index * size, size), size)


def copies_in(chunks, held, sems):
    rows, columns = chunks[0].shape
    blocks = held.shape[0] // rows
    return [
        pltpu.make_async_copy(
            chunk,
            held.at[pl.ds(number % blocks * rows, rows), pl.ds(number // blocks * columns, columns)],
            sems.at[number],
        )
        for number, chunk in enumerate(chunks)
    ]


def fill_zero(total, size):
    @pl.loop(0, total.shape[1] // size)
    def _(block):
        total[:, column_block(block, size)] = jnp.zeros((total.shape[0], size), total.dtype)


def write_out(total, held, outs, sems, size):
    @pl.loop(0, total.shape[1] // size)
    def _(block):
        columns = column_block(block, size)
        held[:, columns] = total[:, columns].astype(held.dtype)

    copies = []
    for number, out in enumerate(outs):
        rows = out.shape[0]
        copies.append(
            pltpu.make_async_copy(held.at[pl.ds(number * rows, rows), :], out, sems.at[number])
        )
    for copy in copies:
        copy.start()
    for copy in copies:
        copy.wait()


def hidden_kernel(chunk_count, wait_count, per, size, up_ref, *refs):
    chunks = refs[:chunk_count]
    low_half, up_weight, low_out = refs[chunk_count : chunk_count + 3]
    hidden, slope, held, in_sems = refs[chunk_count + 3 + wait_count :]
    up_slots = up_weight.shape[1]

    @pl.when(pl.program_id(0) == 0)
    def _():
        copies = copies_in(chunks, held, in_sems)
        for copy in copies:
            copy.start()
        for copy in copies:
            copy.wait()

    for inner in range(per):
        first = (pl.program_id(0) * per + inner) * up_slots
        picked = [held[:, column_block(up_ref[first + slot], size)] for slot in range(up_slots)]
        weights = [up_weight[inner, slot] for slot in range(up_slots)]
        before = dot_nn(
            jnp.concatenate(picked + [low_half[...]], axis=1),
            jnp.concatenate(weights + [low_out[:, inner * size : (inner + 1) * size]], axis=0),
        )
        square = before * before
        bent = jnp.tanh(GELU_SCALE * before * (1.0 + GELU_CUBE * square))
        half = 0.5 * (1.0 + bent)
        hidden[inner] = (before * half).astype(BF16)
        slope[inner] = half + 0.5 * before * (1.0 - bent * bent) * (
            GELU_SCALE * (1.0 + 3.0 * GELU_CUBE * square)
        )


def pieces_kernel(out_count, wait_count, per, size, down_ref, live_ref, *refs):
    hidden, down_weight = refs[:2]
    first_out = 2 + wait_count
    outs = refs[first_out : first_out + out_count]
    held, total, out_sems = refs[first_out + out_count :]
    down_slots = down_weight.shape[1]

    @pl.when(pl.program_id(0) == 0)
    def _():
        fill_zero(total, size)

    for inner in range(per):
        step = pl.program_id(0) * per + inner
        weights = [
            jnp.where(slot < live_ref[step], down_weight[inner, slot], jnp.zeros((), BF16))
            for slot in range(down_slots)
        ]
        pieces = dot_nn(hidden[inner], jnp.concatenate(weights, axis=1))
        for slot in range(down_slots):
            columns = column_block(down_ref[step * down_slots + slot], size)
            total[:, columns] += pieces[:, slot * size : (slot + 1) * size]

    @pl.when(pl.program_id(0) == pl.num_programs(0) - 1)
    def _():
        write_out(total, held, outs, out_sems, size)


def back_kernel(chunk_count, wait_count, per, size, down_ref, live_ref, *refs):
    chunks = refs[:chunk_count]
    slope, down_weight, low_out = refs[chunk_count : chunk_count + 3]
    back_half, back_low, held, sems = refs[chunk_count + 3 + wait_count :]
    down_slots = down_weight.shape[1]

    @pl.when(pl.program_id(0) == 0)
    def _():
        copies = copies_in(chunks, held, sems)
        for copy in copies:
            copy.start()
        back_low[...] = jnp.zeros(back_low.shape, F32)
        for copy in copies:
            copy.wait()

    backs = []
    for inner in range(per):
        step = pl.program_id(0) * per + inner
        wanted = [
            held[:, column_block(down_ref[step * down_slots + slot], size)]
            for slot in range(down_slots)
        ]
        weights = [
            jnp.where(slot < live_ref[step], down_weight[inner, slot], jnp.zeros((), BF16))
            for slot in range(down_slots)
        ]
        back_hidden = dot_nt(jnp.concatenate(wanted, axis=1), jnp.concatenate(weights, axis=1))
        back = (back_hidden * slope[inner]).astype(BF16)
        back_half[inner] = back
        backs.append(back)
    back_low[...] += dot_nt(jnp.concatenate(backs, axis=1), low_out[...])


def load_all(chunks, held, sems):
    @pl.when(pl.program_id(0) == 0)
    def _():
        copies = copies_in(chunks, held, sems)
        for copy in copies:
            copy.start()
        for copy in copies:
            copy.wait()


def write_groups(groups, outs, per, make):
    first = 0
    for number, (length, way) in enumerate(groups):
        steps = length // per
        inside = (pl.program_id(0) >= first) & (pl.program_id(0) < first + steps)

        @pl.when(inside)
        def _(number=number, way=way):
            own, send, passed = outs[3 * number : 3 * number + 3]
            for inner in range(per):
                for slot in range(own.shape[1]):
                    own[inner, slot] = make(inner, slot, 0)
                    passed[inner, slot] = make(inner, slot, 3 - way).astype(BF16)
                    send[0, inner, slot] = make(inner, slot, way).astype(BF16)
                    send[1, inner, slot] = make(inner, slot, 3).astype(BF16)

        first += steps


def down_kernel(
    chunk_count, wait_count, first_step, per, groups, size, down_ref, live_ref, quarter_ref, *refs
):
    chunks = refs[:chunk_count]
    hidden = refs[chunk_count]
    outs = refs[chunk_count + 1 + wait_count : -3]
    held, part, sems = refs[-3:]
    slots, rows = outs[0].shape[1:3]
    load_all(chunks, held, sems)
    step = first_step + pl.program_id(0) * per
    for inner in range(per):
        wanted = [
            held[:, column_block(down_ref[(step + inner) * slots + slot], size)]
            for slot in range(slots)
        ]
        part[inner] = dot_tn(hidden[inner], jnp.concatenate(wanted, axis=1))

    def make(inner, slot, which):
        keep = (slot < live_ref[step + inner]).astype(F32)
        first = pl.multiple_of(quarter_ref[which] * rows, rows)
        return part[inner, pl.ds(first, rows), slot * size : (slot + 1) * size] * keep

    write_groups(groups, outs, per, make)


def up_kernel(chunk_count, wait_count, first_step, per, groups, size, up_ref, quarter_ref, *refs):
    chunks = refs[:chunk_count]
    low_half, back_half = refs[chunk_count : chunk_count + 2]
    outs = refs[chunk_count + 2 + wait_count : -3]
    held, part, sems = refs[-3:]
    slots, rows = outs[0].shape[1] - 1, outs[0].shape[2]
    load_all(chunks, held, sems)
    step = first_step + pl.program_id(0) * per
    for inner in range(per):
        picked = [
            held[:, column_block(up_ref[(step + inner) * slots + slot], size)]
            for slot in range(slots)
        ]
        part[inner] = dot_tn(jnp.concatenate(picked + [low_half[...]], axis=1), back_half[inner])

    def make(inner, slot, which):
        first = pl.multiple_of(quarter_ref[which] * rows + slot * size, rows)
        return part[inner, pl.ds(first, rows), :]

    write_groups(groups, outs, per, make)


def spread_kernel(out_count, wait_count, per, size, up_ref, rank_ref, *refs):
    back_half, up_weight, back_low, low_in = refs[:4]
    first_out = 4 + wait_count
    outs = refs[first_out : first_out + out_count]
    held, total, out_sems = refs[first_out + out_count :]
    up_slots = up_weight.shape[1]

    @pl.when(pl.program_id(0) == 0)
    def _():
        fill_zero(total, size)
        first = rank_ref[0] * (low_in.shape[0] // size)

        @pl.loop(0, low_in.shape[0] // size)
        def _(block):
            rows = pl.ds(pl.multiple_of(block * size, size), size)
            side = dot_nt(back_low[...], low_in[rows, :])
            total[:, column_block(first + block, size)] = side

    for inner in range(per):
        step = pl.program_id(0) * per + inner
        weights = jnp.concatenate([up_weight[inner, slot] for slot in range(up_slots)], axis=0)
        spread = dot_nt(back_half[inner], weights)
        for slot in range(up_slots):
            columns = column_block(up_ref[step * up_slots + slot], size)
            total[:, columns] += spread[:, slot * size : (slot + 1) * size]

    @pl.when(pl.program_id(0) == pl.num_programs(0) - 1)
    def _():
        write_out(total, held, outs, out_sems, size)


def whole_spec(array):
    zeros = (0,) * array.ndim
    return pl.BlockSpec(array.shape, lambda i, *_: zeros)


def any_spec():
    return pl.BlockSpec(memory_space=pl.ANY)


def block_spec(array, per, first=0):
    rest = (0,) * (array.ndim - 1)
    return pl.BlockSpec((per,) + array.shape[1:], lambda i, *_: (i + first // per,) + rest)


def blocks_per_step(count, most):
    return max(per for per in range(1, most + 1) if count % per == 0)


def params():
    return pltpu.CompilerParams(
        dimension_semantics=("arbitrary",), vmem_limit_bytes=VMEM_LIMIT
    )


def shape(dims, dtype):
    return jax.ShapeDtypeStruct(dims, dtype)


def run_hidden(scalars, chunks, low_half, up_weight, low_out, waits, size):
    count, tok_total, width = up_weight.shape[0], low_half.shape[0], chunks[0].shape[1]
    per = blocks_per_step(count, PER_HIDDEN)
    hidden = shape((count, tok_total, size), BF16)
    slope = shape((count, tok_total, size), F32)
    return pl.pallas_call(
        functools.partial(hidden_kernel, len(chunks), len(waits), per, size),
        out_shape=[hidden, slope],
        grid_spec=pltpu.PrefetchScalarGridSpec(
            num_scalar_prefetch=len(scalars),
            grid=(count // per,),
            in_specs=[any_spec()] * len(chunks)
            + [
                whole_spec(low_half),
                block_spec(up_weight, per),
                pl.BlockSpec((low_out.shape[0], per * size), lambda i, *_: (0, i)),
            ]
            + [any_spec()] * len(waits),
            out_specs=[block_spec(hidden, per), block_spec(slope, per)],
            scratch_shapes=[
                pltpu.VMEM((tok_total, width), BF16),
                pltpu.SemaphoreType.DMA((len(chunks),)),
            ],
        ),
        compiler_params=params(),
        cost_estimate=COST,
        name="hidden",
    )(*scalars, *chunks, low_half, up_weight, low_out, *waits)


def run_pieces(scalars, hidden, down_weight, waits, out_shapes, width, size):
    count, tok_total = hidden.shape[:2]
    per = blocks_per_step(count, PER_PIECES)
    return pl.pallas_call(
        functools.partial(pieces_kernel, len(out_shapes), len(waits), per, size),
        out_shape=[shape(dims, BF16) for dims in out_shapes],
        grid_spec=pltpu.PrefetchScalarGridSpec(
            num_scalar_prefetch=len(scalars),
            grid=(count // per,),
            in_specs=[block_spec(hidden, per), block_spec(down_weight, per)] + [any_spec()] * len(waits),
            out_specs=[any_spec()] * len(out_shapes),
            scratch_shapes=[
                pltpu.VMEM((tok_total, width), BF16),
                pltpu.VMEM((tok_total, width), F32),
                pltpu.SemaphoreType.DMA((len(out_shapes),)),
            ],
        ),
        compiler_params=params(),
        cost_estimate=COST,
        name="pieces",
    )(*scalars, hidden, down_weight, *waits)


def run_back(scalars, chunks, slope, down_weight, low_out, waits, width, size):
    count, tok_total = slope.shape[:2]
    per = blocks_per_step(count, PER_BACK)
    back_half = shape((count, tok_total, size), BF16)
    back_low = shape((tok_total, low_out.shape[0]), F32)
    return pl.pallas_call(
        functools.partial(back_kernel, len(chunks), len(waits), per, size),
        out_shape=[back_half, back_low],
        grid_spec=pltpu.PrefetchScalarGridSpec(
            num_scalar_prefetch=len(scalars),
            grid=(count // per,),
            in_specs=[any_spec()] * len(chunks)
            + [
                block_spec(slope, per),
                block_spec(down_weight, per),
                pl.BlockSpec((low_out.shape[0], per * size), lambda i, *_: (0, i)),
            ]
            + [any_spec()] * len(waits),
            out_specs=[block_spec(back_half, per), whole_spec(back_low)],
            scratch_shapes=[
                pltpu.VMEM((tok_total, width), BF16),
                pltpu.SemaphoreType.DMA((len(chunks),)),
            ],
        ),
        compiler_params=params(),
        cost_estimate=COST,
        name="back",
    )(*scalars, *chunks, slope, down_weight, low_out, *waits)


def run_gradients(
    kernel, scalars, chunks, whole, blocks, waits, first, groups, slots, part_shape, parts, width
):
    per = min(blocks_per_step(length, PER_GRADIENTS) for length, _ in groups)
    tok_total, size = blocks.shape[1:]
    rows = size // parts
    outs, specs, step = [], [], 0
    for length, _ in groups:
        last = length // per - 1

        def place(i, start=step, last=last):
            return jnp.clip(i - start, 0, last)

        outs += [
            shape((length, slots, rows, size), F32),
            shape((2, length, slots, rows, size), BF16),
            shape((length, slots, rows, size), BF16),
        ]
        one = pl.BlockSpec((per, slots, rows, size), lambda i, *_, at=place: (at(i), 0, 0, 0))
        two = pl.BlockSpec((2, per, slots, rows, size), lambda i, *_, at=place: (0, at(i), 0, 0, 0))
        specs += [one, two, one]
        step += length // per
    results = pl.pallas_call(
        functools.partial(kernel, len(chunks), len(waits), first, per, groups, size),
        out_shape=outs,
        grid_spec=pltpu.PrefetchScalarGridSpec(
            num_scalar_prefetch=len(scalars),
            grid=(step,),
            in_specs=[any_spec()] * len(chunks)
            + [whole_spec(array) for array in whole]
            + [block_spec(blocks, per, first)]
            + [any_spec()] * len(waits),
            out_specs=specs,
            scratch_shapes=[
                pltpu.VMEM((tok_total, width), BF16),
                pltpu.VMEM((per,) + part_shape, F32),
                pltpu.SemaphoreType.DMA((len(chunks),)),
            ],
        ),
        compiler_params=params(),
        cost_estimate=COST,
        name=kernel.__name__,
    )(*scalars, *chunks, *whole, blocks, *waits)
    return [results[3 * number : 3 * number + 3] for number in range(len(groups))]


def run_spread(scalars, back_half, up_weight, back_low, low_in, waits, out_shapes, width, size):
    count, tok_total = back_half.shape[:2]
    per = blocks_per_step(count, PER_SPREAD)
    return pl.pallas_call(
        functools.partial(spread_kernel, len(out_shapes), len(waits), per, size),
        out_shape=[shape(dims, BF16) for dims in out_shapes],
        grid_spec=pltpu.PrefetchScalarGridSpec(
            num_scalar_prefetch=len(scalars),
            grid=(count // per,),
            in_specs=[
                block_spec(back_half, per),
                block_spec(up_weight, per),
                whole_spec(back_low),
                whole_spec(low_in),
            ]
            + [any_spec()] * len(waits),
            out_specs=[any_spec()] * len(out_shapes),
            scratch_shapes=[
                pltpu.VMEM((tok_total, width), BF16),
                pltpu.VMEM((tok_total, width), F32),
                pltpu.SemaphoreType.DMA((len(out_shapes),)),
            ],
        ),
        compiler_params=params(),
        cost_estimate=COST,
        name="spread",
    )(*scalars, back_half, up_weight, back_low, low_in, *waits)


def pass_kernel(half_count, *refs):
    out, first = refs[-1], 0
    for half in range(half_count):
        passed, got = refs[2 * half : 2 * half + 2]
        length = passed.shape[0]
        out[first : first + length] = (passed[...].astype(F32) + got[0].astype(F32)).astype(BF16)
        first += length


def run_pass(halves):
    length = sum(passed.shape[0] for passed, _ in halves)
    out = shape((length,) + halves[0][0].shape[1:], BF16)
    specs = []
    for passed, got in halves:
        specs += [
            whole_spec(passed),
            pl.BlockSpec((1,) + got.shape[1:], lambda i: (1, 0, 0, 0, 0)),
        ]
    return pl.pallas_call(
        functools.partial(pass_kernel, len(halves)),
        out_shape=out,
        grid=(1,),
        in_specs=specs,
        out_specs=whole_spec(out),
        compiler_params=params(),
        cost_estimate=COST,
        name="pass_on",
    )(*[array for pair in halves for array in pair])


def add_kernel(*refs):
    total = refs[0][...].astype(F32)
    for part in refs[1:-1]:
        total = total + part[...].astype(F32)
    refs[-1][...] = total.astype(BF16)


def run_add(arrays):
    rows, width = arrays[0].shape
    steps = 2 if width % 256 == 0 else 1
    spec = pl.BlockSpec((rows, width // steps), lambda i: (0, i))
    return pl.pallas_call(
        add_kernel,
        out_shape=shape((rows, width), BF16),
        grid=(steps,),
        in_specs=[spec] * len(arrays),
        out_specs=spec,
        compiler_params=params(),
        cost_estimate=COST,
        name="add_rows",
    )(*arrays)


def low_kernel(chunk_count, place_ref, *refs):
    chunks, out = refs[: 2 * chunk_count], refs[-1]
    weight, other_weight = refs[2 * chunk_count : 2 * chunk_count + 2]
    own = jnp.concatenate([chunk[...] for chunk in chunks[:chunk_count]], axis=0)
    other = jnp.concatenate([chunk[...] for chunk in chunks[chunk_count:]], axis=0)
    out[...] = dot_nn(own, weight[...]) + dot_nn(other, other_weight[...])


def run_low(places, chunks, weight, other_weight, waits):
    rows, columns = chunks[0].shape[0], weight.shape[0]
    out = shape((len(chunks) * rows, weight.shape[1]), F32)
    return pl.pallas_call(
        functools.partial(low_kernel, len(chunks)),
        out_shape=out,
        grid_spec=pltpu.PrefetchScalarGridSpec(
            num_scalar_prefetch=1,
            grid=(1,),
            in_specs=[pl.BlockSpec((rows, columns), lambda i, at: (0, at[0]))] * len(chunks)
            + [pl.BlockSpec((rows, columns), lambda i, at: (0, at[1]))] * len(chunks)
            + [whole_spec(weight), whole_spec(other_weight)]
            + [any_spec()] * len(waits),
            out_specs=whole_spec(out),
        ),
        compiler_params=params(),
        cost_estimate=COST,
        name="low_part",
    )(places, *chunks, *chunks, weight, other_weight, *waits)


def side_kernel(place_ref, *refs):
    back_low, out = refs[-2:]
    columns = jnp.concatenate([chunk[...] for chunk in refs[:-2]], axis=0)
    out[...] = dot_tn(columns, back_low[...]).astype(BF16)


def run_side(places, chunks, back_low, col_width):
    rows = chunks[0].shape[0]
    out = shape((col_width, back_low.shape[1]), BF16)
    return pl.pallas_call(
        side_kernel,
        out_shape=out,
        grid_spec=pltpu.PrefetchScalarGridSpec(
            num_scalar_prefetch=1,
            grid=(1,),
            in_specs=[pl.BlockSpec((rows, col_width), lambda i, at: (0, at[0]))] * len(chunks)
            + [whole_spec(back_low)],
            out_specs=whole_spec(out),
        ),
        compiler_params=params(),
        cost_estimate=COST,
        name="low_in_part",
    )(places, *chunks, back_low)


def sum_kernel(places, own_count, *refs):
    out, first = refs[-1], 0
    for number, (last, start) in enumerate(places):
        own, got = refs[2 * number : 2 * number + 2]
        length = own.shape[0]
        total = own[...] + got[0].astype(F32)
        if last is not None:
            total = total + refs[2 * own_count + last][start : start + length].astype(F32)
        out[first : first + length] = total
        first += length


def run_sum(parts, gots, lasts=()):
    pairs = [
        (own[0], got, number, half * own[0].shape[0])
        for half, (part, gots_here) in enumerate(zip(parts, gots))
        for number, (own, got) in enumerate(zip(part, gots_here))
    ]
    places = [(number, start) if lasts else (None, 0) for _, _, number, start in pairs]
    specs, arrays = [], []
    for own, got, _, _ in pairs:
        specs += [
            whole_spec(own),
            pl.BlockSpec((1,) + got.shape[1:], lambda i: (0, 0, 0, 0, 0)),
        ]
        arrays += [own, got]
    specs += [whole_spec(last) for last in lasts]
    length = sum(own.shape[0] for own, _, _, _ in pairs)
    out = shape((length,) + pairs[0][0].shape[1:], F32)
    return pl.pallas_call(
        functools.partial(sum_kernel, places, len(pairs)),
        out_shape=out,
        grid=(1,),
        in_specs=specs,
        out_specs=whole_spec(out),
        compiler_params=params(),
        cost_estimate=COST,
        name="sums",
    )(*arrays, *lasts)


def finish_kernel(group_count, *refs):
    before = refs[0]
    lasts = refs[1 : 1 + group_count]
    blocks, side = refs[1 + group_count :]
    size = blocks.shape[3]
    for number, last in enumerate(lasts):

        @pl.when(pl.program_id(0) % group_count == number)
        def _(last=last):
            for block in range(blocks.shape[0]):
                total = before[block] + last[block].astype(F32)
                blocks[block] = total[:-1]
                side[:, block * size : (block + 1) * size] = total[-1]


def run_finish(before, lasts, group):
    count, slots, rows, size = before.shape
    part = (group, slots, rows, size)
    return pl.pallas_call(
        functools.partial(finish_kernel, len(lasts)),
        out_shape=[shape((count, slots - 1, rows, size), F32), shape((rows, count * size), F32)],
        grid=(count // group,),
        in_specs=[pl.BlockSpec(part, lambda i: (i, 0, 0, 0))]
        + [pl.BlockSpec(part, lambda i: (i // len(lasts), 0, 0, 0))] * len(lasts),
        out_specs=[
            pl.BlockSpec((group, slots - 1, rows, size), lambda i: (i, 0, 0, 0)),
            pl.BlockSpec((rows, group * size), lambda i: (0, i)),
        ],
        compiler_params=params(),
        cost_estimate=COST,
        name="finish",
    )(before, *lasts)


def fence(values, waits):
    values, waits = list(values), list(waits)
    return list(pl.pallas_call(
        lambda *refs: None,
        out_shape=[shape(value.shape, value.dtype) for value in values],
        in_specs=[any_spec()] * (len(values) + len(waits)),
        out_specs=[any_spec()] * len(values),
        input_output_aliases={number: number for number in range(len(values))},
        compiler_params=pltpu.CompilerParams(vmem_limit_bytes=VMEM_LIMIT),
        cost_estimate=COST,
        name="fence",
    )(*values, *waits))


def local(mp_size, dp_size, tokens, up_blocks, down_blocks, down_live, up_weight, low_in, low_out, down_weight, cotangent):
    count, up_slots, size = up_weight.shape[:3]
    rows, width = tokens.shape
    tok_total = rows * mp_size
    col_width = low_in.shape[0]
    rank = lax.axis_index("mp")
    part = lax.axis_index("dp")
    chips = mp_size // 2
    by_ring = rows % 16 == 0 and chips == 4
    swap = [(i, i ^ 1) for i in range(mp_size)]
    step_x = [(i, i ^ 1) for i in range(dp_size)]
    step_y = [(i, i ^ 2) for i in range(dp_size)]

    up_index = lax.dynamic_slice_in_dim(up_blocks, rank * count, count, 0).reshape(-1)
    down_index = lax.dynamic_slice_in_dim(down_blocks, rank * count, count, 0).reshape(-1)
    live = lax.dynamic_slice_in_dim(down_live, rank * count, count, 0)
    quarters = part ^ jnp.arange(dp_size, dtype=jnp.int32)
    out_shapes = [(rows, width)] * mp_size if by_ring else [(tok_total, width)]

    def swapped(piece):
        return lax.ppermute(piece, "mp", swap)

    def shifted(piece, by):
        return lax.ppermute(piece, "mp", [(i, (i + 2 * by) % mp_size) for i in range(mp_size)])

    def add_round(parts, given, place, *moved):
        return run_add([parts[place % chips], given[place % chips], *moved])

    def scatter_whole(parts):
        whole = parts[0].reshape(mp_size, rows, width)
        return lax.psum_scatter(whole, "mp", scatter_dimension=0)

    def over_dp(value, way):
        return lax.ppermute(value, "dp", step_y if way == 2 else step_x)

    def pass_on(parts, gots):
        return [
            run_pass([(part[n][2], got[n]) for part, got in zip(parts, gots)])
            for n in range(len(groups))
        ]

    def sum_rows(chip_sum):
        sent = chip_sum.astype(BF16)
        total = chip_sum
        for by in range(1, chips):
            got = shifted(sent, by)
            total = total + jnp.roll(got, by * rows, axis=0).astype(F32)
        same = total.astype(BF16)
        return same, jnp.concatenate([same, swapped(same)], 0)

    def sum_whole(partial):
        low = lax.psum_scatter(partial, "mp", scatter_dimension=0, tiled=True).astype(BF16)
        return lax.all_gather(low, "mp", axis=0, tiled=True)

    def take_columns(piece, place):
        return lax.dynamic_slice_in_dim(piece, place * col_width, col_width, 1)

    if by_ring:
        places = jnp.stack([rank, rank ^ 1]).astype(jnp.int32)
        other_low = swapped(low_in)
        x_same, x_other = [tokens], []
        y_same, y_other = [cotangent], [swapped(cotangent)]
        for step in range(chips):
            if step < chips - 1:
                if step == 2:
                    x_same[2] = fence(x_same[2:], x_other + y_other + [other_low])[0]
                x_same.append(shifted(x_same[step], 1))
                x_other.append(swapped(x_same[step]))
        x_other.append(swapped(x_same[-1]))
        x_chunks = x_same + x_other
        low_same, low_half = sum_rows(
            run_low(places, x_same, low_in, other_low, x_other[2:3])
        )
        arriving = shifted(cotangent, 1)
        arrived = fence([arriving], [low_same])[0]
        y_same.append(arrived)
        y_other.append(swapped(arrived))
        arriving = shifted(arrived, 1)
    else:
        x_chunks = [lax.all_gather(tokens, "mp", axis=0, tiled=True)]
        y_chunks = [lax.all_gather(cotangent, "mp", axis=0, tiled=True)]
        low = jnp.dot(take_columns(x_chunks[0], rank), low_in, preferred_element_type=F32)
        low_half = sum_whole(low)
    hidden, slope = run_hidden((up_index,), x_chunks, low_half, up_weight, low_out, [], size)
    if by_ring:
        arrived, hidden = fence([arriving, hidden], y_other + [slope])
        y_same.append(arrived)
        y_other.append(swapped(arrived))
        arriving = shifted(arrived, 1)
    mixed_parts = list(
        run_pieces((down_index, live), hidden, down_weight, [], out_shapes, width, size)
    )
    if by_ring:
        arrived, *mixed_parts = fence([arriving] + mixed_parts, y_other)
        y_same.append(arrived)
        y_other.append(swapped(arrived))
        y_chunks = y_same + y_other
        mixed_given = [None, swapped(mixed_parts[chips + 1])]

    down_slots = down_weight.shape[1]
    if count % 4 == 0:
        groups = ((count // 4, 2), (count // 4, 1))
        starts = (0, count // 2)
    else:
        groups, starts = ((count, 2),), (0,)

    def down_part(start, waits):
        return run_gradients(
            down_kernel, (down_index, live, quarters), y_chunks, [], hidden, waits, start, groups,
            down_slots, (size, down_slots * size), dp_size, width,
        )

    def up_part(start, waits):
        return run_gradients(
            up_kernel, (up_index, quarters), x_chunks, [low_half], back_half, waits, start, groups,
            up_slots + 1, ((up_slots + 1) * size, size), dp_size, width,
        )

    def send_round(parts, moving, waits, give=()):
        here = [part[1] for part in parts]
        sent = fence(here + moving + list(give), waits)
        got = [over_dp(value, way) for value, (_, way) in zip(sent, groups)]
        rest = sent[len(here) :]
        moved = [shifted(value, 1) for value in rest[: len(moving)]]
        return sent[0], got, moved, [swapped(value) for value in rest[len(moving) :]]

    down_parts = [down_part(starts[0], [])]
    give, moving = mixed_parts[chips + 2 :] if by_ring else [], []
    token, got, _, given = send_round(
        down_parts[0], [], [y_other[-1], mixed_given[1]] if by_ring else [], give
    )
    if by_ring:
        moving = [shifted(add_round(mixed_parts, mixed_given, 1), 1)]
    down_got = [got]
    back_half, back_low = run_back(
        (down_index, live), y_chunks, slope, down_weight, low_out, [token], width, size
    )
    if len(starts) > 1:
        down_parts.append(down_part(starts[1], [back_half]))
    if by_ring:
        mixed_given += given
        moving = [add_round(mixed_parts, mixed_given, 2, moving[0])]
        waits = down_got[0] + moving + given + [down_parts[-1][0][0]]
        back_low = fence([back_low], waits)[0]
        half = tok_total // 2
        _, back_low = sum_rows(back_low[:half] + swapped(back_low[half:]))
    else:
        back_low = sum_whole(back_low)
    if len(starts) > 1:
        give = mixed_parts[chips : chips + 1] if by_ring else []
        token, got, moving, given = send_round(
            down_parts[1], moving, down_got[0] + [back_low], give
        )
        down_got.append(got)

    up_parts, waits = [], [token]
    for start in starts:
        up_parts.append(up_part(start, waits))
        waits = [up_parts[-1][0][0]]
    if by_ring:
        mixed_given[0] = given[0]
        moving = [add_round(mixed_parts, mixed_given, 3, moving[0])]
        waits = waits + given
    token, got, moving, _ = send_round(up_parts[0], moving, down_got[-1] + waits)
    up_got = [got]
    input_parts = list(
        run_spread(
            (up_index, rank.reshape(1)),
            back_half, up_weight, back_low, low_in, [token], out_shapes, width, size,
        )
    )
    if by_ring:
        low_in_part = run_side(places, x_chunks, back_low, col_width)
    else:
        low_in_part = lax.dot_general(
            take_columns(x_chunks[0], rank), back_low, (((0,), (0,)), ((), ())),
            preferred_element_type=F32,
        ).astype(BF16)
    down_onward = pass_on(down_parts, down_got)
    waits, give = up_got[0] + down_onward + [low_in_part], []
    if by_ring:
        mixed = add_round(mixed_parts, mixed_given, chips, moving[0])
        waits, give = waits + [mixed], input_parts[chips + 1 : chips + 3]
    else:
        mixed, input_grad = scatter_whole(mixed_parts), scatter_whole(input_parts)
    if len(starts) > 1:
        token, got, _, given = send_round(up_parts[1], [], waits, give)
        up_got.append(got)
    if by_ring:
        input_given = [None] + given
        moving = [shifted(add_round(input_parts, input_given, 1), 1)]
        moving = [add_round(input_parts, input_given, 2, moving[0])]

    def last_round(onward, moving, waits, give=()):
        sent = fence(onward + moving + list(give), waits)
        last = [over_dp(value, 3 - way) for value, (_, way) in zip(sent, groups)]
        rest = sent[len(groups) :]
        moved = [shifted(value, 1) for value in rest[: len(moving)]]
        return last, moved, [swapped(value) for value in rest[len(moving) :]]

    give = [input_parts[chips + 3]] if by_ring else []
    down_last, moving, given = last_round(down_onward, moving, up_got[-1], give)
    if by_ring:
        input_given.append(given[0])
        moving = [add_round(input_parts, input_given, 3, moving[0])]
        give = [input_parts[chips]]
    up_last, moving, given = last_round(pass_on(up_parts, up_got), moving, down_last, give)
    if by_ring:
        input_given[0] = given[0]
        input_grad = add_round(input_parts, input_given, chips, moving[0])

    low_in_grad = lax.psum_scatter(
        low_in_part, "dp", scatter_dimension=1, tiled=True
    ).astype(F32)
    down_grad = run_sum(down_parts, down_got, down_last)
    up_grad, low_out_grad = run_finish(
        run_sum(up_parts, up_got), up_last, count // (len(starts) * len(groups))
    )
    return (mixed, input_grad, up_grad, down_grad, low_out_grad, low_in_grad)


def solution(mesh):
    return jax.shard_map(
        functools.partial(local, mesh.shape["mp"], mesh.shape["dp"]),
        mesh=mesh,
        in_specs=(
            P(("dp", "mp"), None),
            P(),
            P(),
            P(),
            P("mp", None, None, None),
            P("mp", None),
            P(None, "mp"),
            P("mp", None, None, None),
            P(("dp", "mp"), None),
        ),
        out_specs=(
            P(("dp", "mp"), None),
            P(("dp", "mp"), None),
            P("mp", None, "dp", None),
            P("mp", None, "dp", None),
            P("dp", "mp"),
            P("mp", "dp"),
        ),
        check_vma=False,
    )
```

```python
import functools

import jax
import jax.numpy as jnp
from jax import lax
from jax.experimental import pallas as pl
from jax.experimental.pallas import tpu as pltpu
from jax.sharding import PartitionSpec as P

F32 = jnp.float32
BF16 = jnp.bfloat16
GELU_SCALE = 0.7978845608028654
GELU_CUBE = 0.044715
PER_HIDDEN, PER_PIECES, PER_BACK, PER_GRADIENTS, PER_SPREAD = 4, 6, 4, 4, 6
COST = pl.CostEstimate(flops=1, bytes_accessed=1, transcendentals=0)
VMEM_LIMIT = 60 * 1024 * 1024


def dot_nn(a, b):
    return lax.dot_general(a, b, (((1,), (0,)), ((), ())), preferred_element_type=F32)


def dot_nt(a, b):
    return lax.dot_general(a, b, (((1,), (1,)), ((), ())), preferred_element_type=F32)


def dot_tn(a, b):
    return lax.dot_general(a, b, (((0,), (0,)), ((), ())), preferred_element_type=F32)


def column_block(index, size):
    return pl.ds(pl.multiple_of(index * size, size), size)


def copies_in(chunks, held, sems):
    rows, columns = chunks[0].shape
    blocks = held.shape[0] // rows
    return [
        pltpu.make_async_copy(
            chunk,
            held.at[pl.ds(number % blocks * rows, rows), pl.ds(number // blocks * columns, columns)],
            sems.at[number],
        )
        for number, chunk in enumerate(chunks)
    ]


def fill_zero(total, size):
    @pl.loop(0, total.shape[1] // size)
    def _(block):
        total[:, column_block(block, size)] = jnp.zeros((total.shape[0], size), total.dtype)


def write_out(total, held, outs, sems, size):
    @pl.loop(0, total.shape[1] // size)
    def _(block):
        columns = column_block(block, size)
        held[:, columns] = total[:, columns].astype(held.dtype)

    copies = []
    for number, out in enumerate(outs):
        rows = out.shape[0]
        copies.append(
            pltpu.make_async_copy(held.at[pl.ds(number * rows, rows), :], out, sems.at[number])
        )
    for copy in copies:
        copy.start()
    for copy in copies:
        copy.wait()


def hidden_kernel(chunk_count, wait_count, per, size, up_ref, *refs):
    chunks = refs[:chunk_count]
    low_half, up_weight, low_out = refs[chunk_count : chunk_count + 3]
    hidden, slope, held, in_sems = refs[chunk_count + 3 + wait_count :]
    up_slots = up_weight.shape[1]

    @pl.when(pl.program_id(0) == 0)
    def _():
        copies = copies_in(chunks, held, in_sems)
        for copy in copies:
            copy.start()
        for copy in copies:
            copy.wait()

    for inner in range(per):
        first = (pl.program_id(0) * per + inner) * up_slots
        picked = [held[:, column_block(up_ref[first + slot], size)] for slot in range(up_slots)]
        weights = [up_weight[inner, slot] for slot in range(up_slots)]
        before = dot_nn(
            jnp.concatenate(picked + [low_half[...]], axis=1),
            jnp.concatenate(weights + [low_out[:, inner * size : (inner + 1) * size]], axis=0),
        )
        square = before * before
        bent = jnp.tanh(GELU_SCALE * before * (1.0 + GELU_CUBE * square))
        half = 0.5 * (1.0 + bent)
        hidden[inner] = (before * half).astype(BF16)
        slope[inner] = half + 0.5 * before * (1.0 - bent * bent) * (
            GELU_SCALE * (1.0 + 3.0 * GELU_CUBE * square)
        )


def pieces_kernel(out_count, wait_count, per, size, down_ref, live_ref, *refs):
    hidden, down_weight = refs[:2]
    first_out = 2 + wait_count
    outs = refs[first_out : first_out + out_count]
    held, total, out_sems = refs[first_out + out_count :]
    down_slots = down_weight.shape[1]

    @pl.when(pl.program_id(0) == 0)
    def _():
        fill_zero(total, size)

    for inner in range(per):
        step = pl.program_id(0) * per + inner
        weights = [
            jnp.where(slot < live_ref[step], down_weight[inner, slot], jnp.zeros((), BF16))
            for slot in range(down_slots)
        ]
        pieces = dot_nn(hidden[inner], jnp.concatenate(weights, axis=1))
        for slot in range(down_slots):
            columns = column_block(down_ref[step * down_slots + slot], size)
            total[:, columns] += pieces[:, slot * size : (slot + 1) * size]

    @pl.when(pl.program_id(0) == pl.num_programs(0) - 1)
    def _():
        write_out(total, held, outs, out_sems, size)


def back_kernel(chunk_count, wait_count, per, size, down_ref, live_ref, *refs):
    chunks = refs[:chunk_count]
    slope, down_weight, low_out = refs[chunk_count : chunk_count + 3]
    back_half, back_low, held, sems = refs[chunk_count + 3 + wait_count :]
    down_slots = down_weight.shape[1]

    @pl.when(pl.program_id(0) == 0)
    def _():
        copies = copies_in(chunks, held, sems)
        for copy in copies:
            copy.start()
        back_low[...] = jnp.zeros(back_low.shape, F32)
        for copy in copies:
            copy.wait()

    backs = []
    for inner in range(per):
        step = pl.program_id(0) * per + inner
        wanted = [
            held[:, column_block(down_ref[step * down_slots + slot], size)]
            for slot in range(down_slots)
        ]
        weights = [
            jnp.where(slot < live_ref[step], down_weight[inner, slot], jnp.zeros((), BF16))
            for slot in range(down_slots)
        ]
        back_hidden = dot_nt(jnp.concatenate(wanted, axis=1), jnp.concatenate(weights, axis=1))
        back = (back_hidden * slope[inner]).astype(BF16)
        back_half[inner] = back
        backs.append(back)
    back_low[...] += dot_nt(jnp.concatenate(backs, axis=1), low_out[...])


def load_all(chunks, held, sems):
    @pl.when(pl.program_id(0) == 0)
    def _():
        copies = copies_in(chunks, held, sems)
        for copy in copies:
            copy.start()
        for copy in copies:
            copy.wait()


def write_groups(groups, outs, per, make):
    first = 0
    for number, (length, way) in enumerate(groups):
        steps = length // per
        inside = (pl.program_id(0) >= first) & (pl.program_id(0) < first + steps)

        @pl.when(inside)
        def _(number=number, way=way):
            own, send, passed = outs[3 * number : 3 * number + 3]
            for inner in range(per):
                for slot in range(own.shape[1]):
                    own[inner, slot] = make(inner, slot, 0)
                    passed[inner, slot] = make(inner, slot, 3 - way).astype(BF16)
                    send[0, inner, slot] = make(inner, slot, way).astype(BF16)
                    send[1, inner, slot] = make(inner, slot, 3).astype(BF16)

        first += steps


def down_kernel(
    chunk_count, wait_count, first_step, per, groups, size, down_ref, live_ref, quarter_ref, *refs
):
    chunks = refs[:chunk_count]
    hidden = refs[chunk_count]
    outs = refs[chunk_count + 1 + wait_count : -3]
    held, part, sems = refs[-3:]
    slots, rows = outs[0].shape[1:3]
    load_all(chunks, held, sems)
    step = first_step + pl.program_id(0) * per
    for inner in range(per):
        wanted = [
            held[:, column_block(down_ref[(step + inner) * slots + slot], size)]
            for slot in range(slots)
        ]
        part[inner] = dot_tn(hidden[inner], jnp.concatenate(wanted, axis=1))

    def make(inner, slot, which):
        keep = (slot < live_ref[step + inner]).astype(F32)
        first = pl.multiple_of(quarter_ref[which] * rows, rows)
        return part[inner, pl.ds(first, rows), slot * size : (slot + 1) * size] * keep

    write_groups(groups, outs, per, make)


def up_kernel(chunk_count, wait_count, first_step, per, groups, size, up_ref, quarter_ref, *refs):
    chunks = refs[:chunk_count]
    low_half, back_half = refs[chunk_count : chunk_count + 2]
    outs = refs[chunk_count + 2 + wait_count : -3]
    held, part, sems = refs[-3:]
    slots, rows = outs[0].shape[1] - 1, outs[0].shape[2]
    load_all(chunks, held, sems)
    step = first_step + pl.program_id(0) * per
    for inner in range(per):
        picked = [
            held[:, column_block(up_ref[(step + inner) * slots + slot], size)]
            for slot in range(slots)
        ]
        part[inner] = dot_tn(jnp.concatenate(picked + [low_half[...]], axis=1), back_half[inner])

    def make(inner, slot, which):
        first = pl.multiple_of(quarter_ref[which] * rows + slot * size, rows)
        return part[inner, pl.ds(first, rows), :]

    write_groups(groups, outs, per, make)


def spread_kernel(out_count, wait_count, per, size, up_ref, rank_ref, *refs):
    back_half, up_weight, back_low, low_in = refs[:4]
    first_out = 4 + wait_count
    outs = refs[first_out : first_out + out_count]
    held, total, out_sems = refs[first_out + out_count :]
    up_slots = up_weight.shape[1]

    @pl.when(pl.program_id(0) == 0)
    def _():
        fill_zero(total, size)
        first = rank_ref[0] * (low_in.shape[0] // size)

        @pl.loop(0, low_in.shape[0] // size)
        def _(block):
            rows = pl.ds(pl.multiple_of(block * size, size), size)
            side = dot_nt(back_low[...], low_in[rows, :])
            total[:, column_block(first + block, size)] = side

    for inner in range(per):
        step = pl.program_id(0) * per + inner
        weights = jnp.concatenate([up_weight[inner, slot] for slot in range(up_slots)], axis=0)
        spread = dot_nt(back_half[inner], weights)
        for slot in range(up_slots):
            columns = column_block(up_ref[step * up_slots + slot], size)
            total[:, columns] += spread[:, slot * size : (slot + 1) * size]

    @pl.when(pl.program_id(0) == pl.num_programs(0) - 1)
    def _():
        write_out(total, held, outs, out_sems, size)


def whole_spec(array):
    zeros = (0,) * array.ndim
    return pl.BlockSpec(array.shape, lambda i, *_: zeros)


def any_spec():
    return pl.BlockSpec(memory_space=pl.ANY)


def block_spec(array, per, first=0):
    rest = (0,) * (array.ndim - 1)
    return pl.BlockSpec((per,) + array.shape[1:], lambda i, *_: (i + first // per,) + rest)


def blocks_per_step(count, most):
    return max(per for per in range(1, most + 1) if count % per == 0)


def params():
    return pltpu.CompilerParams(
        dimension_semantics=("arbitrary",), vmem_limit_bytes=VMEM_LIMIT
    )


def shape(dims, dtype):
    return jax.ShapeDtypeStruct(dims, dtype)


def run_hidden(scalars, chunks, low_half, up_weight, low_out, waits, size):
    count, tok_total, width = up_weight.shape[0], low_half.shape[0], chunks[0].shape[1]
    per = blocks_per_step(count, PER_HIDDEN)
    hidden = shape((count, tok_total, size), BF16)
    slope = shape((count, tok_total, size), F32)
    return pl.pallas_call(
        functools.partial(hidden_kernel, len(chunks), len(waits), per, size),
        out_shape=[hidden, slope],
        grid_spec=pltpu.PrefetchScalarGridSpec(
            num_scalar_prefetch=len(scalars),
            grid=(count // per,),
            in_specs=[any_spec()] * len(chunks)
            + [
                whole_spec(low_half),
                block_spec(up_weight, per),
                pl.BlockSpec((low_out.shape[0], per * size), lambda i, *_: (0, i)),
            ]
            + [any_spec()] * len(waits),
            out_specs=[block_spec(hidden, per), block_spec(slope, per)],
            scratch_shapes=[
                pltpu.VMEM((tok_total, width), BF16),
                pltpu.SemaphoreType.DMA((len(chunks),)),
            ],
        ),
        compiler_params=params(),
        cost_estimate=COST,
        name="hidden",
    )(*scalars, *chunks, low_half, up_weight, low_out, *waits)


def run_pieces(scalars, hidden, down_weight, waits, out_shapes, width, size):
    count, tok_total = hidden.shape[:2]
    per = blocks_per_step(count, PER_PIECES)
    return pl.pallas_call(
        functools.partial(pieces_kernel, len(out_shapes), len(waits), per, size),
        out_shape=[shape(dims, BF16) for dims in out_shapes],
        grid_spec=pltpu.PrefetchScalarGridSpec(
            num_scalar_prefetch=len(scalars),
            grid=(count // per,),
            in_specs=[block_spec(hidden, per), block_spec(down_weight, per)] + [any_spec()] * len(waits),
            out_specs=[any_spec()] * len(out_shapes),
            scratch_shapes=[
                pltpu.VMEM((tok_total, width), BF16),
                pltpu.VMEM((tok_total, width), F32),
                pltpu.SemaphoreType.DMA((len(out_shapes),)),
            ],
        ),
        compiler_params=params(),
        cost_estimate=COST,
        name="pieces",
    )(*scalars, hidden, down_weight, *waits)


def run_back(scalars, chunks, slope, down_weight, low_out, waits, width, size):
    count, tok_total = slope.shape[:2]
    per = blocks_per_step(count, PER_BACK)
    back_half = shape((count, tok_total, size), BF16)
    back_low = shape((tok_total, low_out.shape[0]), F32)
    return pl.pallas_call(
        functools.partial(back_kernel, len(chunks), len(waits), per, size),
        out_shape=[back_half, back_low],
        grid_spec=pltpu.PrefetchScalarGridSpec(
            num_scalar_prefetch=len(scalars),
            grid=(count // per,),
            in_specs=[any_spec()] * len(chunks)
            + [
                block_spec(slope, per),
                block_spec(down_weight, per),
                pl.BlockSpec((low_out.shape[0], per * size), lambda i, *_: (0, i)),
            ]
            + [any_spec()] * len(waits),
            out_specs=[block_spec(back_half, per), whole_spec(back_low)],
            scratch_shapes=[
                pltpu.VMEM((tok_total, width), BF16),
                pltpu.SemaphoreType.DMA((len(chunks),)),
            ],
        ),
        compiler_params=params(),
        cost_estimate=COST,
        name="back",
    )(*scalars, *chunks, slope, down_weight, low_out, *waits)


def run_gradients(
    kernel, scalars, chunks, whole, blocks, waits, first, groups, slots, part_shape, parts, width
):
    per = min(blocks_per_step(length, PER_GRADIENTS) for length, _ in groups)
    tok_total, size = blocks.shape[1:]
    rows = size // parts
    outs, specs, step = [], [], 0
    for length, _ in groups:
        last = length // per - 1

        def place(i, start=step, last=last):
            return jnp.clip(i - start, 0, last)

        outs += [
            shape((length, slots, rows, size), F32),
            shape((2, length, slots, rows, size), BF16),
            shape((length, slots, rows, size), BF16),
        ]
        one = pl.BlockSpec((per, slots, rows, size), lambda i, *_, at=place: (at(i), 0, 0, 0))
        two = pl.BlockSpec((2, per, slots, rows, size), lambda i, *_, at=place: (0, at(i), 0, 0, 0))
        specs += [one, two, one]
        step += length // per
    results = pl.pallas_call(
        functools.partial(kernel, len(chunks), len(waits), first, per, groups, size),
        out_shape=outs,
        grid_spec=pltpu.PrefetchScalarGridSpec(
            num_scalar_prefetch=len(scalars),
            grid=(step,),
            in_specs=[any_spec()] * len(chunks)
            + [whole_spec(array) for array in whole]
            + [block_spec(blocks, per, first)]
            + [any_spec()] * len(waits),
            out_specs=specs,
            scratch_shapes=[
                pltpu.VMEM((tok_total, width), BF16),
                pltpu.VMEM((per,) + part_shape, F32),
                pltpu.SemaphoreType.DMA((len(chunks),)),
            ],
        ),
        compiler_params=params(),
        cost_estimate=COST,
        name=kernel.__name__,
    )(*scalars, *chunks, *whole, blocks, *waits)
    return [results[3 * number : 3 * number + 3] for number in range(len(groups))]


def run_spread(scalars, back_half, up_weight, back_low, low_in, waits, out_shapes, width, size):
    count, tok_total = back_half.shape[:2]
    per = blocks_per_step(count, PER_SPREAD)
    return pl.pallas_call(
        functools.partial(spread_kernel, len(out_shapes), len(waits), per, size),
        out_shape=[shape(dims, BF16) for dims in out_shapes],
        grid_spec=pltpu.PrefetchScalarGridSpec(
            num_scalar_prefetch=len(scalars),
            grid=(count // per,),
            in_specs=[
                block_spec(back_half, per),
                block_spec(up_weight, per),
                whole_spec(back_low),
                whole_spec(low_in),
            ]
            + [any_spec()] * len(waits),
            out_specs=[any_spec()] * len(out_shapes),
            scratch_shapes=[
                pltpu.VMEM((tok_total, width), BF16),
                pltpu.VMEM((tok_total, width), F32),
                pltpu.SemaphoreType.DMA((len(out_shapes),)),
            ],
        ),
        compiler_params=params(),
        cost_estimate=COST,
        name="spread",
    )(*scalars, back_half, up_weight, back_low, low_in, *waits)


def pass_kernel(half_count, *refs):
    out, first = refs[-1], 0
    for half in range(half_count):
        passed, got = refs[2 * half : 2 * half + 2]
        length = passed.shape[0]
        out[first : first + length] = (passed[...].astype(F32) + got[0].astype(F32)).astype(BF16)
        first += length


def run_pass(halves):
    length = sum(passed.shape[0] for passed, _ in halves)
    out = shape((length,) + halves[0][0].shape[1:], BF16)
    specs = []
    for passed, got in halves:
        specs += [
            whole_spec(passed),
            pl.BlockSpec((1,) + got.shape[1:], lambda i: (1, 0, 0, 0, 0)),
        ]
    return pl.pallas_call(
        functools.partial(pass_kernel, len(halves)),
        out_shape=out,
        grid=(1,),
        in_specs=specs,
        out_specs=whole_spec(out),
        compiler_params=params(),
        cost_estimate=COST,
        name="pass_on",
    )(*[array for pair in halves for array in pair])


def add_kernel(*refs):
    total = refs[0][...].astype(F32)
    for part in refs[1:-1]:
        total = total + part[...].astype(F32)
    refs[-1][...] = total.astype(BF16)


def run_add(arrays):
    rows, width = arrays[0].shape
    steps = 2 if width % 256 == 0 else 1
    spec = pl.BlockSpec((rows, width // steps), lambda i: (0, i))
    return pl.pallas_call(
        add_kernel,
        out_shape=shape((rows, width), BF16),
        grid=(steps,),
        in_specs=[spec] * len(arrays),
        out_specs=spec,
        compiler_params=params(),
        cost_estimate=COST,
        name="add_rows",
    )(*arrays)


def low_kernel(chunk_count, place_ref, *refs):
    chunks, out = refs[: 2 * chunk_count], refs[-1]
    weight, other_weight = refs[2 * chunk_count : 2 * chunk_count + 2]
    own = jnp.concatenate([chunk[...] for chunk in chunks[:chunk_count]], axis=0)
    other = jnp.concatenate([chunk[...] for chunk in chunks[chunk_count:]], axis=0)
    out[...] = dot_nn(own, weight[...]) + dot_nn(other, other_weight[...])


def run_low(places, chunks, weight, other_weight, waits):
    rows, columns = chunks[0].shape[0], weight.shape[0]
    out = shape((len(chunks) * rows, weight.shape[1]), F32)
    return pl.pallas_call(
        functools.partial(low_kernel, len(chunks)),
        out_shape=out,
        grid_spec=pltpu.PrefetchScalarGridSpec(
            num_scalar_prefetch=1,
            grid=(1,),
            in_specs=[pl.BlockSpec((rows, columns), lambda i, at: (0, at[0]))] * len(chunks)
            + [pl.BlockSpec((rows, columns), lambda i, at: (0, at[1]))] * len(chunks)
            + [whole_spec(weight), whole_spec(other_weight)]
            + [any_spec()] * len(waits),
            out_specs=whole_spec(out),
        ),
        compiler_params=params(),
        cost_estimate=COST,
        name="low_part",
    )(places, *chunks, *chunks, weight, other_weight, *waits)


def side_kernel(place_ref, *refs):
    back_low, out = refs[-2:]
    columns = jnp.concatenate([chunk[...] for chunk in refs[:-2]], axis=0)
    out[...] = dot_tn(columns, back_low[...]).astype(BF16)


def run_side(places, chunks, back_low, col_width):
    rows = chunks[0].shape[0]
    out = shape((col_width, back_low.shape[1]), BF16)
    return pl.pallas_call(
        side_kernel,
        out_shape=out,
        grid_spec=pltpu.PrefetchScalarGridSpec(
            num_scalar_prefetch=1,
            grid=(1,),
            in_specs=[pl.BlockSpec((rows, col_width), lambda i, at: (0, at[0]))] * len(chunks)
            + [whole_spec(back_low)],
            out_specs=whole_spec(out),
        ),
        compiler_params=params(),
        cost_estimate=COST,
        name="low_in_part",
    )(places, *chunks, back_low)


def sum_kernel(places, own_count, *refs):
    out, first = refs[-1], 0
    for number, (last, start) in enumerate(places):
        own, got = refs[2 * number : 2 * number + 2]
        length = own.shape[0]
        total = own[...] + got[0].astype(F32)
        if last is not None:
            total = total + refs[2 * own_count + last][start : start + length].astype(F32)
        out[first : first + length] = total
        first += length


def run_sum(parts, gots, lasts=()):
    pairs, firsts = [], [0] * len(parts[0])
    for part, gots_here in zip(parts, gots):
        for number, (own, got) in enumerate(zip(part, gots_here)):
            pairs.append((own[0], got, number, firsts[number]))
            firsts[number] += own[0].shape[0]
    places = [(number, start) if lasts else (None, 0) for _, _, number, start in pairs]
    specs, arrays = [], []
    for own, got, _, _ in pairs:
        specs += [
            whole_spec(own),
            pl.BlockSpec((1,) + got.shape[1:], lambda i: (0, 0, 0, 0, 0)),
        ]
        arrays += [own, got]
    specs += [whole_spec(last) for last in lasts]
    length = sum(own.shape[0] for own, _, _, _ in pairs)
    out = shape((length,) + pairs[0][0].shape[1:], F32)
    return pl.pallas_call(
        functools.partial(sum_kernel, places, len(pairs)),
        out_shape=out,
        grid=(1,),
        in_specs=specs,
        out_specs=whole_spec(out),
        compiler_params=params(),
        cost_estimate=COST,
        name="sums",
    )(*arrays, *lasts)


def finish_kernel(group_count, *refs):
    before = refs[0]
    lasts = refs[1 : 1 + group_count]
    blocks, side = refs[1 + group_count :]
    size = blocks.shape[3]
    for number, last in enumerate(lasts):

        @pl.when(pl.program_id(0) % group_count == number)
        def _(last=last):
            for block in range(blocks.shape[0]):
                total = before[block] + last[block].astype(F32)
                blocks[block] = total[:-1]
                side[:, block * size : (block + 1) * size] = total[-1]


def run_finish(before, lasts, group):
    count, slots, rows, size = before.shape
    part = (group, slots, rows, size)
    return pl.pallas_call(
        functools.partial(finish_kernel, len(lasts)),
        out_shape=[shape((count, slots - 1, rows, size), F32), shape((rows, count * size), F32)],
        grid=(count // group,),
        in_specs=[pl.BlockSpec(part, lambda i: (i, 0, 0, 0))]
        + [pl.BlockSpec(part, lambda i: (i // len(lasts), 0, 0, 0))] * len(lasts),
        out_specs=[
            pl.BlockSpec((group, slots - 1, rows, size), lambda i: (i, 0, 0, 0)),
            pl.BlockSpec((rows, group * size), lambda i: (0, i)),
        ],
        compiler_params=params(),
        cost_estimate=COST,
        name="finish",
    )(before, *lasts)


def fence(values, waits):
    values, waits = list(values), list(waits)
    return list(pl.pallas_call(
        lambda *refs: None,
        out_shape=[shape(value.shape, value.dtype) for value in values],
        in_specs=[any_spec()] * (len(values) + len(waits)),
        out_specs=[any_spec()] * len(values),
        input_output_aliases={number: number for number in range(len(values))},
        compiler_params=pltpu.CompilerParams(vmem_limit_bytes=VMEM_LIMIT),
        cost_estimate=COST,
        name="fence",
    )(*values, *waits))


def local(mp_size, dp_size, tokens, up_blocks, down_blocks, down_live, up_weight, low_in, low_out, down_weight, cotangent):
    count, up_slots, size = up_weight.shape[:3]
    rows, width = tokens.shape
    tok_total = rows * mp_size
    col_width = low_in.shape[0]
    rank = lax.axis_index("mp")
    part = lax.axis_index("dp")
    chips = mp_size // 2
    by_ring = rows % 16 == 0 and chips == 4
    swap = [(i, i ^ 1) for i in range(mp_size)]
    step_x = [(i, i ^ 1) for i in range(dp_size)]
    step_y = [(i, i ^ 2) for i in range(dp_size)]

    up_index = lax.dynamic_slice_in_dim(up_blocks, rank * count, count, 0).reshape(-1)
    down_index = lax.dynamic_slice_in_dim(down_blocks, rank * count, count, 0).reshape(-1)
    live = lax.dynamic_slice_in_dim(down_live, rank * count, count, 0)
    quarters = part ^ jnp.arange(dp_size, dtype=jnp.int32)
    out_shapes = [(rows, width)] * mp_size if by_ring else [(tok_total, width)]

    def swapped(piece):
        return lax.ppermute(piece, "mp", swap)

    def shifted(piece, by):
        return lax.ppermute(piece, "mp", [(i, (i + 2 * by) % mp_size) for i in range(mp_size)])

    def add_round(parts, given, place, *moved):
        return run_add([parts[place % chips], given[place % chips], *moved])

    def scatter_whole(parts):
        whole = parts[0].reshape(mp_size, rows, width)
        return lax.psum_scatter(whole, "mp", scatter_dimension=0)

    def over_dp(value, way):
        return lax.ppermute(value, "dp", step_y if way == 2 else step_x)

    def pass_on(parts, gots):
        return [
            run_pass([(part[n][2], got[n]) for part, got in zip(parts, gots)])
            for n in range(len(groups))
        ]

    def all_rows(total):
        same = total.astype(BF16)
        other, early = swapped(same), (chips - 1) * rows
        pieces = in_rows([same[:early], same[early:]], [other[:early], other[early:]])
        return same, jnp.concatenate(pieces, 0)

    def sum_rows(chip_sum):
        sent = chip_sum.astype(BF16)
        total = chip_sum
        for by in range(1, chips):
            got = shifted(sent, by)
            total = total + jnp.roll(got, by * rows, axis=0).astype(F32)
        return all_rows(total)

    def sum_rows_in_pairs(chip_sum, waits):
        near = [(i, i ^ 2) for i in range(mp_size)]
        far = [(i, i ^ 4) for i in range(mp_size)]
        got = fence([lax.ppermute(chip_sum.astype(BF16), "mp", near)], waits)[0].astype(F32)
        even = (rank // 2) % 2 == 0
        got = jnp.where(even, jnp.roll(got, -rows, axis=0), jnp.roll(got, rows, axis=0))
        pair_sum = chip_sum + got
        got = lax.ppermute(pair_sum.astype(BF16), "mp", far).astype(F32)
        return all_rows(pair_sum + jnp.roll(got, 2 * rows, axis=0))

    def sum_whole(partial):
        low = lax.psum_scatter(partial, "mp", scatter_dimension=0, tiled=True).astype(BF16)
        return lax.all_gather(low, "mp", axis=0, tiled=True)

    def in_rows(same, other):
        return same[:-1] + other[:-1] + same[-1:] + other[-1:]

    def by_core(parts):
        early = chips - 1
        return parts[:early] + parts[-2:-1] + parts[early:-2] + parts[-1:]

    def take_columns(piece, place):
        return lax.dynamic_slice_in_dim(piece, place * col_width, col_width, 1)

    if by_ring:
        places = jnp.stack([rank, rank ^ 1]).astype(jnp.int32)
        other_low = swapped(low_in)
        x_same, x_other = [tokens], []
        y_same, y_other = [cotangent], [swapped(cotangent)]
        for step in range(chips):
            if step < chips - 1:
                if step == 2:
                    x_same[2] = fence(x_same[2:], x_other + y_other + [other_low])[0]
                x_same.append(shifted(x_same[step], 1))
                x_other.append(swapped(x_same[step]))
        x_other.append(swapped(x_same[-1]))
        x_chunks = in_rows(x_same, x_other)
        low_same, low_half = sum_rows(
            run_low(places, x_same, low_in, other_low, x_other[2:3])
        )
        arriving = shifted(cotangent, 1)
        arrived = fence([arriving], [low_same])[0]
        y_same.append(arrived)
        y_other.append(swapped(arrived))
        arriving = shifted(arrived, 1)
    else:
        x_chunks = [lax.all_gather(tokens, "mp", axis=0, tiled=True)]
        y_chunks = [lax.all_gather(cotangent, "mp", axis=0, tiled=True)]
        low = jnp.dot(take_columns(x_chunks[0], rank), low_in, preferred_element_type=F32)
        low_half = sum_whole(low)
    hidden, slope = run_hidden((up_index,), x_chunks, low_half, up_weight, low_out, [], size)
    if by_ring:
        arrived, hidden = fence([arriving, hidden], y_other + [slope])
        y_same.append(arrived)
        y_other.append(swapped(arrived))
        arriving = shifted(arrived, 1)
    mixed_parts = list(
        run_pieces((down_index, live), hidden, down_weight, [], out_shapes, width, size)
    )
    if by_ring:
        mixed_parts = by_core(mixed_parts)
        arrived, *mixed_parts = fence([arriving] + mixed_parts, y_other)
        y_same.append(arrived)
        y_other.append(swapped(arrived))
        y_chunks = in_rows(y_same, y_other)
        mixed_given = [None] + [swapped(piece) for piece in mixed_parts[chips + 1 :]]

    down_slots = down_weight.shape[1]
    if count % 12 == 0:
        groups, starts = ((count // 4, 2), (count // 4, 1)), (0, count // 2)
        down_groups = ((count // 6, 2), (count // 6, 1), (count // 3, 2), (count // 3, 1))
    else:
        groups, starts = ((count, 2),), (0,)
        down_groups = groups

    def up_part(start, waits):
        return run_gradients(
            up_kernel, (up_index, quarters), x_chunks, [low_half], back_half, waits, start, groups,
            up_slots + 1, ((up_slots + 1) * size, size), dp_size, width,
        )

    def send_round(parts, moving, waits, give=()):
        here = [part[1] for part in parts]
        sent = fence(here + moving + list(give), waits)
        got = [over_dp(value, way) for value, (_, way) in zip(sent, groups)]
        rest = sent[len(here) :]
        moved = [shifted(value, 1) for value in rest[: len(moving)]]
        return sent[0], got, moved, [swapped(value) for value in rest[len(moving) :]]

    down_all = run_gradients(
        down_kernel, (down_index, live, quarters), y_chunks, [], hidden, [], 0, down_groups,
        down_slots, (size, down_slots * size), dp_size, width,
    )
    down_parts = [down_all[n : n + len(groups)] for n in range(0, len(down_all), len(groups))]
    waits = [y_other[-1]] + mixed_given[1:] if by_ring else []
    token, got, _, _ = send_round(down_parts[0], [], waits)
    down_got, moving = [got], []
    if by_ring:
        moved = shifted(add_round(mixed_parts, mixed_given, 1), 1)
        moving = [add_round(mixed_parts, mixed_given, 2, moved)]
    back_half, back_low = run_back(
        (down_index, live), y_chunks, slope, down_weight, low_out, [token], width, size
    )
    if len(down_parts) > 1:
        here = [part[1] for part in down_parts[1]]
        token, *sent = fence([back_low] + here + moving, down_got[0])
        back_low, moving = token, sent[len(here) :]
        down_got.append([over_dp(value, way) for value, (_, way) in zip(sent, groups)])
    up_parts, waits = [], [token]
    for start in starts:
        up_parts.append(up_part(start, waits))
        waits = [up_parts[-1][0][0]]
    if by_ring:
        low = by_core([back_low[n * rows : (n + 1) * rows] for n in range(mp_size)])
        chip_sum = jnp.concatenate(low[:chips], 0) + swapped(jnp.concatenate(low[chips:], 0))
        _, back_low = sum_rows_in_pairs(chip_sum, waits)
        moving = [add_round(mixed_parts, mixed_given, 3, shifted(moving[0], 1))]
    else:
        back_low = sum_whole(back_low)
    give = [mixed_parts[chips]] if by_ring else []
    token, got, moving, given = send_round(
        up_parts[0], moving, down_got[-1] + waits + [back_low], give
    )
    up_got = [got]
    if by_ring:
        mixed_given[0] = given[0]
    input_parts = list(
        run_spread(
            (up_index, rank.reshape(1)),
            back_half, up_weight, back_low, low_in, [token], out_shapes, width, size,
        )
    )
    if by_ring:
        low_in_part = run_side(places, x_chunks, back_low, col_width)
    else:
        low_in_part = lax.dot_general(
            take_columns(x_chunks[0], rank), back_low, (((0,), (0,)), ((), ())),
            preferred_element_type=F32,
        ).astype(BF16)
    down_onward = pass_on(down_parts, down_got)
    waits, give = up_got[0] + down_onward + [low_in_part], []
    if by_ring:
        input_parts = by_core(input_parts)
        mixed = add_round(mixed_parts, mixed_given, chips, moving[0])
        waits, give = waits + [mixed], input_parts[chips + 1 : chips + 3]
    else:
        mixed, input_grad = scatter_whole(mixed_parts), scatter_whole(input_parts)
    if len(starts) > 1:
        token, got, _, given = send_round(up_parts[1], [], waits, give)
        up_got.append(got)
    if by_ring:
        input_given = [None] + given
        moving = [shifted(add_round(input_parts, input_given, 1), 1)]
        moving = [add_round(input_parts, input_given, 2, moving[0])]

    def last_round(onward, moving, waits, give=()):
        sent = fence(onward + moving + list(give), waits)
        last = [over_dp(value, 3 - way) for value, (_, way) in zip(sent, groups)]
        rest = sent[len(groups) :]
        moved = [shifted(value, 1) for value in rest[: len(moving)]]
        return last, moved, [swapped(value) for value in rest[len(moving) :]]

    give = [input_parts[chips + 3]] if by_ring else []
    down_last, moving, given = last_round(down_onward, moving, up_got[-1], give)
    if by_ring:
        input_given.append(given[0])
        moving = [add_round(input_parts, input_given, 3, moving[0])]
        give = [input_parts[chips]]
    up_last, moving, given = last_round(pass_on(up_parts, up_got), moving, down_last, give)
    if by_ring:
        input_given[0] = given[0]
        input_grad = add_round(input_parts, input_given, chips, moving[0])

    low_in_grad = lax.psum_scatter(
        low_in_part, "dp", scatter_dimension=1, tiled=True
    ).astype(F32)
    down_grad = run_sum(down_parts, down_got, down_last)
    up_grad, low_out_grad = run_finish(
        run_sum(up_parts, up_got), up_last, count // (len(starts) * len(groups))
    )
    return (mixed, input_grad, up_grad, down_grad, low_out_grad, low_in_grad)


def solution(mesh):
    return jax.shard_map(
        functools.partial(local, mesh.shape["mp"], mesh.shape["dp"]),
        mesh=mesh,
        in_specs=(
            P(("dp", "mp"), None),
            P(),
            P(),
            P(),
            P("mp", None, None, None),
            P("mp", None),
            P(None, "mp"),
            P("mp", None, None, None),
            P(("dp", "mp"), None),
        ),
        out_specs=(
            P(("dp", "mp"), None),
            P(("dp", "mp"), None),
            P("mp", None, "dp", None),
            P("mp", None, "dp", None),
            P("dp", "mp"),
            P("mp", "dp"),
        ),
        check_vma=False,
    )
```

```python
import functools

import jax
import jax.numpy as jnp
from jax import lax
from jax.experimental import pallas as pl
from jax.experimental.pallas import tpu as pltpu
from jax.sharding import PartitionSpec as P

F32 = jnp.float32
BF16 = jnp.bfloat16
GELU_SCALE = 0.7978845608028654
GELU_CUBE = 0.044715
PER_HIDDEN, PER_PIECES, PER_BACK, PER_GRADIENTS, PER_SPREAD = 4, 6, 4, 4, 6
COST = pl.CostEstimate(flops=1, bytes_accessed=1, transcendentals=0)
VMEM_LIMIT = 60 * 1024 * 1024


def dot_nn(a, b):
    return lax.dot_general(a, b, (((1,), (0,)), ((), ())), preferred_element_type=F32)


def dot_nt(a, b):
    return lax.dot_general(a, b, (((1,), (1,)), ((), ())), preferred_element_type=F32)


def dot_tn(a, b):
    return lax.dot_general(a, b, (((0,), (0,)), ((), ())), preferred_element_type=F32)


def column_block(index, size):
    return pl.ds(pl.multiple_of(index * size, size), size)


def copies_in(chunks, held, sems):
    rows, columns = chunks[0].shape
    blocks = held.shape[0] // rows
    return [
        pltpu.make_async_copy(
            chunk,
            held.at[pl.ds(number % blocks * rows, rows), pl.ds(number // blocks * columns, columns)],
            sems.at[number],
        )
        for number, chunk in enumerate(chunks)
    ]


def fill_zero(total, size):
    @pl.loop(0, total.shape[1] // size)
    def _(block):
        total[:, column_block(block, size)] = jnp.zeros((total.shape[0], size), total.dtype)


def write_out(total, held, outs, sems, size):
    @pl.loop(0, total.shape[1] // size)
    def _(block):
        columns = column_block(block, size)
        held[:, columns] = total[:, columns].astype(held.dtype)

    copies = []
    for number, out in enumerate(outs):
        rows = out.shape[0]
        copies.append(
            pltpu.make_async_copy(held.at[pl.ds(number * rows, rows), :], out, sems.at[number])
        )
    for copy in copies:
        copy.start()
    for copy in copies:
        copy.wait()


def hidden_kernel(chunk_count, wait_count, per, size, up_ref, *refs):
    chunks = refs[:chunk_count]
    low_half, up_weight, low_out = refs[chunk_count : chunk_count + 3]
    hidden, slope, held, in_sems = refs[chunk_count + 3 + wait_count :]
    up_slots = up_weight.shape[1]

    @pl.when(pl.program_id(0) == 0)
    def _():
        copies = copies_in(chunks, held, in_sems)
        for copy in copies:
            copy.start()
        for copy in copies:
            copy.wait()

    for inner in range(per):
        first = (pl.program_id(0) * per + inner) * up_slots
        picked = [held[:, column_block(up_ref[first + slot], size)] for slot in range(up_slots)]
        weights = [up_weight[inner, slot] for slot in range(up_slots)]
        before = dot_nn(
            jnp.concatenate(picked + [low_half[...]], axis=1),
            jnp.concatenate(weights + [low_out[:, inner * size : (inner + 1) * size]], axis=0),
        )
        square = before * before
        bent = jnp.tanh(GELU_SCALE * before * (1.0 + GELU_CUBE * square))
        half = 0.5 * (1.0 + bent)
        hidden[inner] = (before * half).astype(BF16)
        slope[inner] = half + 0.5 * before * (1.0 - bent * bent) * (
            GELU_SCALE * (1.0 + 3.0 * GELU_CUBE * square)
        )


def pieces_kernel(out_count, wait_count, per, size, down_ref, live_ref, *refs):
    hidden, down_weight = refs[:2]
    first_out = 2 + wait_count
    outs = refs[first_out : first_out + out_count]
    held, total, out_sems = refs[first_out + out_count :]
    down_slots = down_weight.shape[1]

    @pl.when(pl.program_id(0) == 0)
    def _():
        fill_zero(total, size)

    for inner in range(per):
        step = pl.program_id(0) * per + inner
        weights = [
            jnp.where(slot < live_ref[step], down_weight[inner, slot], jnp.zeros((), BF16))
            for slot in range(down_slots)
        ]
        pieces = dot_nn(hidden[inner], jnp.concatenate(weights, axis=1))
        for slot in range(down_slots):
            columns = column_block(down_ref[step * down_slots + slot], size)
            total[:, columns] += pieces[:, slot * size : (slot + 1) * size]

    @pl.when(pl.program_id(0) == pl.num_programs(0) - 1)
    def _():
        write_out(total, held, outs, out_sems, size)


def back_kernel(chunk_count, wait_count, per, size, down_ref, live_ref, *refs):
    chunks = refs[:chunk_count]
    slope, down_weight, low_out = refs[chunk_count : chunk_count + 3]
    back_half, back_low, held, sems = refs[chunk_count + 3 + wait_count :]
    down_slots = down_weight.shape[1]

    @pl.when(pl.program_id(0) == 0)
    def _():
        copies = copies_in(chunks, held, sems)
        for copy in copies:
            copy.start()
        back_low[...] = jnp.zeros(back_low.shape, F32)
        for copy in copies:
            copy.wait()

    backs = []
    for inner in range(per):
        step = pl.program_id(0) * per + inner
        wanted = [
            held[:, column_block(down_ref[step * down_slots + slot], size)]
            for slot in range(down_slots)
        ]
        weights = [
            jnp.where(slot < live_ref[step], down_weight[inner, slot], jnp.zeros((), BF16))
            for slot in range(down_slots)
        ]
        back_hidden = dot_nt(jnp.concatenate(wanted, axis=1), jnp.concatenate(weights, axis=1))
        back = (back_hidden * slope[inner]).astype(BF16)
        back_half[inner] = back
        backs.append(back)
    back_low[...] += dot_nt(jnp.concatenate(backs, axis=1), low_out[...])


def load_all(chunks, held, sems):
    @pl.when(pl.program_id(0) == 0)
    def _():
        copies = copies_in(chunks, held, sems)
        for copy in copies:
            copy.start()
        for copy in copies:
            copy.wait()


def write_groups(groups, outs, per, make):
    first = 0
    for number, (length, way) in enumerate(groups):
        steps = length // per
        inside = (pl.program_id(0) >= first) & (pl.program_id(0) < first + steps)

        @pl.when(inside)
        def _(number=number, way=way):
            own, send, passed = outs[3 * number : 3 * number + 3]
            for inner in range(per):
                for slot in range(own.shape[1]):
                    own[inner, slot] = make(inner, slot, 0)
                    passed[inner, slot] = make(inner, slot, 3 - way).astype(BF16)
                    send[0, inner, slot] = make(inner, slot, way).astype(BF16)
                    send[1, inner, slot] = make(inner, slot, 3).astype(BF16)

        first += steps


def down_kernel(
    chunk_count, wait_count, first_step, per, groups, size, down_ref, live_ref, quarter_ref, *refs
):
    chunks = refs[:chunk_count]
    hidden = refs[chunk_count]
    outs = refs[chunk_count + 1 + wait_count : -3]
    held, part, sems = refs[-3:]
    slots, rows = outs[0].shape[1:3]
    load_all(chunks, held, sems)
    step = first_step + pl.program_id(0) * per
    for inner in range(per):
        wanted = [
            held[:, column_block(down_ref[(step + inner) * slots + slot], size)]
            for slot in range(slots)
        ]
        part[inner] = dot_tn(hidden[inner], jnp.concatenate(wanted, axis=1))

    def make(inner, slot, which):
        keep = (slot < live_ref[step + inner]).astype(F32)
        first = pl.multiple_of(quarter_ref[which] * rows, rows)
        return part[inner, pl.ds(first, rows), slot * size : (slot + 1) * size] * keep

    write_groups(groups, outs, per, make)


def up_kernel(chunk_count, wait_count, first_step, per, groups, size, up_ref, quarter_ref, *refs):
    chunks = refs[:chunk_count]
    low_half, back_half = refs[chunk_count : chunk_count + 2]
    outs = refs[chunk_count + 2 + wait_count : -3]
    held, part, sems = refs[-3:]
    slots, rows = outs[0].shape[1] - 1, outs[0].shape[2]
    load_all(chunks, held, sems)
    step = first_step + pl.program_id(0) * per
    for inner in range(per):
        picked = [
            held[:, column_block(up_ref[(step + inner) * slots + slot], size)]
            for slot in range(slots)
        ]
        part[inner] = dot_tn(jnp.concatenate(picked + [low_half[...]], axis=1), back_half[inner])

    def make(inner, slot, which):
        first = pl.multiple_of(quarter_ref[which] * rows + slot * size, rows)
        return part[inner, pl.ds(first, rows), :]

    write_groups(groups, outs, per, make)


def spread_kernel(out_count, wait_count, per, size, up_ref, rank_ref, *refs):
    back_half, up_weight, back_low, low_in = refs[:4]
    first_out = 4 + wait_count
    outs = refs[first_out : first_out + out_count]
    held, total, out_sems = refs[first_out + out_count :]
    up_slots = up_weight.shape[1]

    @pl.when(pl.program_id(0) == 0)
    def _():
        fill_zero(total, size)
        first = rank_ref[0] * (low_in.shape[0] // size)

        @pl.loop(0, low_in.shape[0] // size)
        def _(block):
            rows = pl.ds(pl.multiple_of(block * size, size), size)
            side = dot_nt(back_low[...], low_in[rows, :])
            total[:, column_block(first + block, size)] = side

    for inner in range(per):
        step = pl.program_id(0) * per + inner
        weights = jnp.concatenate([up_weight[inner, slot] for slot in range(up_slots)], axis=0)
        spread = dot_nt(back_half[inner], weights)
        for slot in range(up_slots):
            columns = column_block(up_ref[step * up_slots + slot], size)
            total[:, columns] += spread[:, slot * size : (slot + 1) * size]

    @pl.when(pl.program_id(0) == pl.num_programs(0) - 1)
    def _():
        write_out(total, held, outs, out_sems, size)


def whole_spec(array):
    zeros = (0,) * array.ndim
    return pl.BlockSpec(array.shape, lambda i, *_: zeros)


def any_spec():
    return pl.BlockSpec(memory_space=pl.ANY)


def block_spec(array, per, first=0):
    rest = (0,) * (array.ndim - 1)
    return pl.BlockSpec((per,) + array.shape[1:], lambda i, *_: (i + first // per,) + rest)


def blocks_per_step(count, most):
    return max(per for per in range(1, most + 1) if count % per == 0)


def params():
    return pltpu.CompilerParams(
        dimension_semantics=("arbitrary",), vmem_limit_bytes=VMEM_LIMIT
    )


def shape(dims, dtype):
    return jax.ShapeDtypeStruct(dims, dtype)


def run_hidden(scalars, chunks, low_half, up_weight, low_out, waits, size):
    count, tok_total, width = up_weight.shape[0], low_half.shape[0], chunks[0].shape[1]
    per = blocks_per_step(count, PER_HIDDEN)
    hidden = shape((count, tok_total, size), BF16)
    slope = shape((count, tok_total, size), F32)
    return pl.pallas_call(
        functools.partial(hidden_kernel, len(chunks), len(waits), per, size),
        out_shape=[hidden, slope],
        grid_spec=pltpu.PrefetchScalarGridSpec(
            num_scalar_prefetch=len(scalars),
            grid=(count // per,),
            in_specs=[any_spec()] * len(chunks)
            + [
                whole_spec(low_half),
                block_spec(up_weight, per),
                pl.BlockSpec((low_out.shape[0], per * size), lambda i, *_: (0, i)),
            ]
            + [any_spec()] * len(waits),
            out_specs=[block_spec(hidden, per), block_spec(slope, per)],
            scratch_shapes=[
                pltpu.VMEM((tok_total, width), BF16),
                pltpu.SemaphoreType.DMA((len(chunks),)),
            ],
        ),
        compiler_params=params(),
        cost_estimate=COST,
        name="hidden",
    )(*scalars, *chunks, low_half, up_weight, low_out, *waits)


def run_pieces(scalars, hidden, down_weight, waits, out_shapes, width, size):
    count, tok_total = hidden.shape[:2]
    per = blocks_per_step(count, PER_PIECES)
    return pl.pallas_call(
        functools.partial(pieces_kernel, len(out_shapes), len(waits), per, size),
        out_shape=[shape(dims, BF16) for dims in out_shapes],
        grid_spec=pltpu.PrefetchScalarGridSpec(
            num_scalar_prefetch=len(scalars),
            grid=(count // per,),
            in_specs=[block_spec(hidden, per), block_spec(down_weight, per)] + [any_spec()] * len(waits),
            out_specs=[any_spec()] * len(out_shapes),
            scratch_shapes=[
                pltpu.VMEM((tok_total, width), BF16),
                pltpu.VMEM((tok_total, width), F32),
                pltpu.SemaphoreType.DMA((len(out_shapes),)),
            ],
        ),
        compiler_params=params(),
        cost_estimate=COST,
        name="pieces",
    )(*scalars, hidden, down_weight, *waits)


def run_back(scalars, chunks, slope, down_weight, low_out, waits, width, size):
    count, tok_total = slope.shape[:2]
    per = blocks_per_step(count, PER_BACK)
    back_half = shape((count, tok_total, size), BF16)
    back_low = shape((tok_total, low_out.shape[0]), F32)
    return pl.pallas_call(
        functools.partial(back_kernel, len(chunks), len(waits), per, size),
        out_shape=[back_half, back_low],
        grid_spec=pltpu.PrefetchScalarGridSpec(
            num_scalar_prefetch=len(scalars),
            grid=(count // per,),
            in_specs=[any_spec()] * len(chunks)
            + [
                block_spec(slope, per),
                block_spec(down_weight, per),
                pl.BlockSpec((low_out.shape[0], per * size), lambda i, *_: (0, i)),
            ]
            + [any_spec()] * len(waits),
            out_specs=[block_spec(back_half, per), whole_spec(back_low)],
            scratch_shapes=[
                pltpu.VMEM((tok_total, width), BF16),
                pltpu.SemaphoreType.DMA((len(chunks),)),
            ],
        ),
        compiler_params=params(),
        cost_estimate=COST,
        name="back",
    )(*scalars, *chunks, slope, down_weight, low_out, *waits)


def run_gradients(
    kernel, scalars, chunks, whole, blocks, waits, first, groups, slots, part_shape, parts, width
):
    per = min(blocks_per_step(length, PER_GRADIENTS) for length, _ in groups)
    tok_total, size = blocks.shape[1:]
    rows = size // parts
    outs, specs, step = [], [], 0
    for length, _ in groups:
        last = length // per - 1

        def place(i, start=step, last=last):
            return jnp.clip(i - start, 0, last)

        outs += [
            shape((length, slots, rows, size), F32),
            shape((2, length, slots, rows, size), BF16),
            shape((length, slots, rows, size), BF16),
        ]
        one = pl.BlockSpec((per, slots, rows, size), lambda i, *_, at=place: (at(i), 0, 0, 0))
        two = pl.BlockSpec((2, per, slots, rows, size), lambda i, *_, at=place: (0, at(i), 0, 0, 0))
        specs += [one, two, one]
        step += length // per
    results = pl.pallas_call(
        functools.partial(kernel, len(chunks), len(waits), first, per, groups, size),
        out_shape=outs,
        grid_spec=pltpu.PrefetchScalarGridSpec(
            num_scalar_prefetch=len(scalars),
            grid=(step,),
            in_specs=[any_spec()] * len(chunks)
            + [whole_spec(array) for array in whole]
            + [block_spec(blocks, per, first)]
            + [any_spec()] * len(waits),
            out_specs=specs,
            scratch_shapes=[
                pltpu.VMEM((tok_total, width), BF16),
                pltpu.VMEM((per,) + part_shape, F32),
                pltpu.SemaphoreType.DMA((len(chunks),)),
            ],
        ),
        compiler_params=params(),
        cost_estimate=COST,
        name=kernel.__name__,
    )(*scalars, *chunks, *whole, blocks, *waits)
    return [results[3 * number : 3 * number + 3] for number in range(len(groups))]


def run_spread(scalars, back_half, up_weight, back_low, low_in, waits, out_shapes, width, size):
    count, tok_total = back_half.shape[:2]
    per = blocks_per_step(count, PER_SPREAD)
    return pl.pallas_call(
        functools.partial(spread_kernel, len(out_shapes), len(waits), per, size),
        out_shape=[shape(dims, BF16) for dims in out_shapes],
        grid_spec=pltpu.PrefetchScalarGridSpec(
            num_scalar_prefetch=len(scalars),
            grid=(count // per,),
            in_specs=[
                block_spec(back_half, per),
                block_spec(up_weight, per),
                whole_spec(back_low),
                whole_spec(low_in),
            ]
            + [any_spec()] * len(waits),
            out_specs=[any_spec()] * len(out_shapes),
            scratch_shapes=[
                pltpu.VMEM((tok_total, width), BF16),
                pltpu.VMEM((tok_total, width), F32),
                pltpu.SemaphoreType.DMA((len(out_shapes),)),
            ],
        ),
        compiler_params=params(),
        cost_estimate=COST,
        name="spread",
    )(*scalars, back_half, up_weight, back_low, low_in, *waits)


def pass_kernel(half_count, *refs):
    out, first = refs[-1], 0
    for half in range(half_count):
        passed, got = refs[2 * half : 2 * half + 2]
        length = passed.shape[0]
        out[first : first + length] = (passed[...].astype(F32) + got[0].astype(F32)).astype(BF16)
        first += length


def run_pass(halves):
    length = sum(passed.shape[0] for passed, _ in halves)
    out = shape((length,) + halves[0][0].shape[1:], BF16)
    specs = []
    for passed, got in halves:
        specs += [
            whole_spec(passed),
            pl.BlockSpec((1,) + got.shape[1:], lambda i: (1, 0, 0, 0, 0)),
        ]
    return pl.pallas_call(
        functools.partial(pass_kernel, len(halves)),
        out_shape=out,
        grid=(1,),
        in_specs=specs,
        out_specs=whole_spec(out),
        compiler_params=params(),
        cost_estimate=COST,
        name="pass_on",
    )(*[array for pair in halves for array in pair])


def add_kernel(*refs):
    total = refs[0][...].astype(F32)
    for part in refs[1:-1]:
        total = total + part[...].astype(F32)
    refs[-1][...] = total.astype(BF16)


def run_add(arrays):
    rows, width = arrays[0].shape
    steps = 2 if width % 256 == 0 else 1
    spec = pl.BlockSpec((rows, width // steps), lambda i: (0, i))
    return pl.pallas_call(
        add_kernel,
        out_shape=shape((rows, width), BF16),
        grid=(steps,),
        in_specs=[spec] * len(arrays),
        out_specs=spec,
        compiler_params=params(),
        cost_estimate=COST,
        name="add_rows",
    )(*arrays)


def low_kernel(chunk_count, place_ref, *refs):
    chunks, out = refs[: 2 * chunk_count], refs[-1]
    weight, other_weight = refs[2 * chunk_count : 2 * chunk_count + 2]
    own = jnp.concatenate([chunk[...] for chunk in chunks[:chunk_count]], axis=0)
    other = jnp.concatenate([chunk[...] for chunk in chunks[chunk_count:]], axis=0)
    out[...] = dot_nn(own, weight[...]) + dot_nn(other, other_weight[...])


def run_low(places, chunks, weight, other_weight, waits):
    rows, columns = chunks[0].shape[0], weight.shape[0]
    out = shape((len(chunks) * rows, weight.shape[1]), F32)
    return pl.pallas_call(
        functools.partial(low_kernel, len(chunks)),
        out_shape=out,
        grid_spec=pltpu.PrefetchScalarGridSpec(
            num_scalar_prefetch=1,
            grid=(1,),
            in_specs=[pl.BlockSpec((rows, columns), lambda i, at: (0, at[0]))] * len(chunks)
            + [pl.BlockSpec((rows, columns), lambda i, at: (0, at[1]))] * len(chunks)
            + [whole_spec(weight), whole_spec(other_weight)]
            + [any_spec()] * len(waits),
            out_specs=whole_spec(out),
        ),
        compiler_params=params(),
        cost_estimate=COST,
        name="low_part",
    )(places, *chunks, *chunks, weight, other_weight, *waits)


def side_kernel(place_ref, *refs):
    back_low, out = refs[-2:]
    columns = jnp.concatenate([chunk[...] for chunk in refs[:-2]], axis=0)
    out[...] = dot_tn(columns, back_low[...]).astype(BF16)


def run_side(places, chunks, back_low, col_width):
    rows = chunks[0].shape[0]
    out = shape((col_width, back_low.shape[1]), BF16)
    return pl.pallas_call(
        side_kernel,
        out_shape=out,
        grid_spec=pltpu.PrefetchScalarGridSpec(
            num_scalar_prefetch=1,
            grid=(1,),
            in_specs=[pl.BlockSpec((rows, col_width), lambda i, at: (0, at[0]))] * len(chunks)
            + [whole_spec(back_low)],
            out_specs=whole_spec(out),
        ),
        compiler_params=params(),
        cost_estimate=COST,
        name="low_in_part",
    )(places, *chunks, back_low)


def sum_kernel(places, own_count, *refs):
    out, first = refs[-1], 0
    for number, (last, start) in enumerate(places):
        own, got = refs[2 * number : 2 * number + 2]
        length = own.shape[0]
        total = own[...] + got[0].astype(F32)
        if last is not None:
            total = total + refs[2 * own_count + last][start : start + length].astype(F32)
        out[first : first + length] = total
        first += length


def run_sum(parts, gots, lasts=()):
    pairs, firsts = [], [0] * len(parts[0])
    for part, gots_here in zip(parts, gots):
        for number, (own, got) in enumerate(zip(part, gots_here)):
            pairs.append((own[0], got, number, firsts[number]))
            firsts[number] += own[0].shape[0]
    places = [(number, start) if lasts else (None, 0) for _, _, number, start in pairs]
    specs, arrays = [], []
    for own, got, _, _ in pairs:
        specs += [
            whole_spec(own),
            pl.BlockSpec((1,) + got.shape[1:], lambda i: (0, 0, 0, 0, 0)),
        ]
        arrays += [own, got]
    specs += [whole_spec(last) for last in lasts]
    length = sum(own.shape[0] for own, _, _, _ in pairs)
    out = shape((length,) + pairs[0][0].shape[1:], F32)
    return pl.pallas_call(
        functools.partial(sum_kernel, places, len(pairs)),
        out_shape=out,
        grid=(1,),
        in_specs=specs,
        out_specs=whole_spec(out),
        compiler_params=params(),
        cost_estimate=COST,
        name="sums",
    )(*arrays, *lasts)


def finish_kernel(group_count, *refs):
    before = refs[0]
    lasts = refs[1 : 1 + group_count]
    blocks, side = refs[1 + group_count :]
    size = blocks.shape[3]
    for number, last in enumerate(lasts):

        @pl.when(pl.program_id(0) % group_count == number)
        def _(last=last):
            for block in range(blocks.shape[0]):
                total = before[block] + last[block].astype(F32)
                blocks[block] = total[:-1]
                side[:, block * size : (block + 1) * size] = total[-1]


def run_finish(before, lasts, group):
    count, slots, rows, size = before.shape
    part = (group, slots, rows, size)
    return pl.pallas_call(
        functools.partial(finish_kernel, len(lasts)),
        out_shape=[shape((count, slots - 1, rows, size), F32), shape((rows, count * size), F32)],
        grid=(count // group,),
        in_specs=[pl.BlockSpec(part, lambda i: (i, 0, 0, 0))]
        + [pl.BlockSpec(part, lambda i: (i // len(lasts), 0, 0, 0))] * len(lasts),
        out_specs=[
            pl.BlockSpec((group, slots - 1, rows, size), lambda i: (i, 0, 0, 0)),
            pl.BlockSpec((rows, group * size), lambda i: (0, i)),
        ],
        compiler_params=params(),
        cost_estimate=COST,
        name="finish",
    )(before, *lasts)


def fence(values, waits):
    values, waits = list(values), list(waits)
    return list(pl.pallas_call(
        lambda *refs: None,
        out_shape=[shape(value.shape, value.dtype) for value in values],
        in_specs=[any_spec()] * (len(values) + len(waits)),
        out_specs=[any_spec()] * len(values),
        input_output_aliases={number: number for number in range(len(values))},
        compiler_params=pltpu.CompilerParams(vmem_limit_bytes=VMEM_LIMIT),
        cost_estimate=COST,
        name="fence",
    )(*values, *waits))


def local(mp_size, dp_size, tokens, up_blocks, down_blocks, down_live, up_weight, low_in, low_out, down_weight, cotangent):
    count, up_slots, size = up_weight.shape[:3]
    rows, width = tokens.shape
    tok_total = rows * mp_size
    col_width = low_in.shape[0]
    rank = lax.axis_index("mp")
    part = lax.axis_index("dp")
    chips = mp_size // 2
    by_ring = rows % 16 == 0 and chips == 4
    swap = [(i, i ^ 1) for i in range(mp_size)]
    step_x = [(i, i ^ 1) for i in range(dp_size)]
    step_y = [(i, i ^ 2) for i in range(dp_size)]

    up_index = lax.dynamic_slice_in_dim(up_blocks, rank * count, count, 0).reshape(-1)
    down_index = lax.dynamic_slice_in_dim(down_blocks, rank * count, count, 0).reshape(-1)
    live = lax.dynamic_slice_in_dim(down_live, rank * count, count, 0)
    quarters = part ^ jnp.arange(dp_size, dtype=jnp.int32)
    out_shapes = [(rows, width)] * mp_size if by_ring else [(tok_total, width)]

    def swapped(piece):
        return lax.ppermute(piece, "mp", swap)

    def shifted(piece, by):
        return lax.ppermute(piece, "mp", [(i, (i + 2 * by) % mp_size) for i in range(mp_size)])

    def add_round(parts, given, place, *moved):
        return run_add([parts[place % chips], given[place % chips], *moved])

    def scatter_whole(parts):
        whole = parts[0].reshape(mp_size, rows, width)
        return lax.psum_scatter(whole, "mp", scatter_dimension=0)

    def over_dp(value, way):
        return lax.ppermute(value, "dp", step_y if way == 2 else step_x)

    def pass_on(parts, gots):
        return [
            run_pass([(part[n][2], got[n]) for part, got in zip(parts, gots)])
            for n in range(len(groups))
        ]

    def all_rows(total):
        same = total.astype(BF16)
        other, early = swapped(same), (chips - 1) * rows
        pieces = in_rows([same[:early], same[early:]], [other[:early], other[early:]])
        return same, jnp.concatenate(pieces, 0)

    def sum_rows(chip_sum):
        sent = chip_sum.astype(BF16)
        total = chip_sum
        for by in range(1, chips):
            got = shifted(sent, by)
            total = total + jnp.roll(got, by * rows, axis=0).astype(F32)
        return all_rows(total)

    def sum_rows_in_pairs(chip_sum, waits):
        near = [(i, i ^ 2) for i in range(mp_size)]
        far = [(i, i ^ 4) for i in range(mp_size)]
        got = fence([lax.ppermute(chip_sum.astype(BF16), "mp", near)], waits)[0].astype(F32)
        even = (rank // 2) % 2 == 0
        got = jnp.where(even, jnp.roll(got, -rows, axis=0), jnp.roll(got, rows, axis=0))
        pair_sum = chip_sum + got
        got = lax.ppermute(pair_sum.astype(BF16), "mp", far).astype(F32)
        return all_rows(pair_sum + jnp.roll(got, 2 * rows, axis=0))

    def sum_whole(partial):
        low = lax.psum_scatter(partial, "mp", scatter_dimension=0, tiled=True).astype(BF16)
        return lax.all_gather(low, "mp", axis=0, tiled=True)

    def in_rows(same, other):
        return same[:-1] + other[:-1] + same[-1:] + other[-1:]

    def by_core(parts):
        early = chips - 1
        return parts[:early] + parts[-2:-1] + parts[early:-2] + parts[-1:]

    def take_columns(piece, place):
        return lax.dynamic_slice_in_dim(piece, place * col_width, col_width, 1)

    if by_ring:
        places = jnp.stack([rank, rank ^ 1]).astype(jnp.int32)
        other_low = swapped(low_in)
        x_same, x_other = [tokens], []
        y_same, y_other = [cotangent], [swapped(cotangent)]
        for step in range(chips):
            if step < chips - 1:
                if step == 2:
                    x_same[2] = fence(x_same[2:], x_other + y_other + [other_low])[0]
                x_same.append(shifted(x_same[step], 1))
                x_other.append(swapped(x_same[step]))
        x_other.append(swapped(x_same[-1]))
        x_chunks = in_rows(x_same, x_other)
        low_same, low_half = sum_rows(
            run_low(places, x_same, low_in, other_low, x_other[2:3])
        )
        arriving = shifted(cotangent, 1)
        arrived = fence([arriving], [low_same])[0]
        y_same.append(arrived)
        y_other.append(swapped(arrived))
        arriving = shifted(arrived, 1)
    else:
        x_chunks = [lax.all_gather(tokens, "mp", axis=0, tiled=True)]
        y_chunks = [lax.all_gather(cotangent, "mp", axis=0, tiled=True)]
        low = jnp.dot(take_columns(x_chunks[0], rank), low_in, preferred_element_type=F32)
        low_half = sum_whole(low)
    hidden, slope = run_hidden((up_index,), x_chunks, low_half, up_weight, low_out, [], size)
    if by_ring:
        arrived, hidden = fence([arriving, hidden], y_other + [slope])
        y_same.append(arrived)
        y_other.append(swapped(arrived))
        arriving = shifted(arrived, 1)
    mixed_parts = list(
        run_pieces((down_index, live), hidden, down_weight, [], out_shapes, width, size)
    )
    if by_ring:
        mixed_parts = by_core(mixed_parts)
        arrived, *mixed_parts = fence([arriving] + mixed_parts, y_other)
        y_same.append(arrived)
        y_other.append(swapped(arrived))
        y_chunks = in_rows(y_same, y_other)
        mixed_given = [None] + [swapped(piece) for piece in mixed_parts[chips + 1 :]]

    down_slots = down_weight.shape[1]
    if count % 12 == 0:
        groups, starts = ((count // 4, 2), (count // 4, 1)), (0, count // 2)
        down_groups = ((count // 6, 2), (count // 6, 1), (count // 3, 2), (count // 3, 1))
    else:
        groups, starts = ((count, 2),), (0,)
        down_groups = groups

    def up_part(start, waits):
        return run_gradients(
            up_kernel, (up_index, quarters), x_chunks, [low_half], back_half, waits, start, groups,
            up_slots + 1, ((up_slots + 1) * size, size), dp_size, width,
        )

    def send_round(parts, moving, waits, give=()):
        here = [part[1] for part in parts]
        sent = fence(here + list(give), waits + moving)
        got = [over_dp(value, way) for value, (_, way) in zip(sent, groups)]
        moved = [shifted(value, 1) for value in moving]
        return sent[0], got, moved, [swapped(value) for value in sent[len(here) :]]

    down_all = run_gradients(
        down_kernel, (down_index, live, quarters), y_chunks, [], hidden, [], 0, down_groups,
        down_slots, (size, down_slots * size), dp_size, width,
    )
    down_parts = [down_all[n : n + len(groups)] for n in range(0, len(down_all), len(groups))]
    waits = [y_other[-1]] + mixed_given[1:] if by_ring else []
    token, got, _, _ = send_round(down_parts[0], [], waits)
    down_got, moving = [got], []
    if by_ring:
        moved = shifted(add_round(mixed_parts, mixed_given, 1), 1)
        moving = [add_round(mixed_parts, mixed_given, 2, moved)]
    back_half, back_low = run_back(
        (down_index, live), y_chunks, slope, down_weight, low_out, [token], width, size
    )
    if len(down_parts) > 1:
        here = [part[1] for part in down_parts[1]]
        token, *sent = fence([back_low] + here, down_got[0] + moving)
        back_low = token
        down_got.append([over_dp(value, way) for value, (_, way) in zip(sent, groups)])
    up_parts = [up_part(starts[0], [token])]
    waits = [up_parts[0][0][0]]
    if by_ring:
        low = by_core([back_low[n * rows : (n + 1) * rows] for n in range(mp_size)])
        chip_sum = jnp.concatenate(low[:chips], 0) + swapped(jnp.concatenate(low[chips:], 0))
        _, back_low = sum_rows_in_pairs(chip_sum, waits)
        moving = [add_round(mixed_parts, mixed_given, 3, shifted(moving[0], 1))]
    else:
        back_low = sum_whole(back_low)
    give = [mixed_parts[chips]] if by_ring else []
    token, got, moving, given = send_round(
        up_parts[0], moving, down_got[-1] + waits + [back_low], give
    )
    up_got = [got]
    if len(starts) > 1:
        up_parts.append(up_part(starts[1], [token]))
    if by_ring:
        mixed_given[0] = given[0]
    input_parts = list(
        run_spread(
            (up_index, rank.reshape(1)),
            back_half, up_weight, back_low, low_in, [token], out_shapes, width, size,
        )
    )
    if by_ring:
        low_in_part = run_side(places, x_chunks, back_low, col_width)
    else:
        low_in_part = lax.dot_general(
            take_columns(x_chunks[0], rank), back_low, (((0,), (0,)), ((), ())),
            preferred_element_type=F32,
        ).astype(BF16)
    down_onward = pass_on(down_parts, down_got)
    waits, give = up_got[0], []
    if by_ring:
        input_parts = by_core(input_parts)
        mixed = add_round(mixed_parts, mixed_given, chips, moving[0])
        waits, give = waits + [mixed], input_parts[chips + 1 : chips + 3]
    else:
        mixed, input_grad = scatter_whole(mixed_parts), scatter_whole(input_parts)
    if len(starts) > 1:
        token, got, _, given = send_round(up_parts[1], [], waits, give)
        up_got.append(got)
    if by_ring:
        input_given = [None] + given
        moving = [shifted(add_round(input_parts, input_given, 1), 1)]
        moving = [add_round(input_parts, input_given, 2, moving[0])]

    def last_round(onward, moving, waits, give=()):
        sent = fence(onward + list(give), waits + moving)
        last = [over_dp(value, 3 - way) for value, (_, way) in zip(sent, groups)]
        moved = [shifted(value, 1) for value in moving]
        return last, moved, [swapped(value) for value in sent[len(groups) :]]

    give = [input_parts[chips + 3]] if by_ring else []
    down_last, moving, given = last_round(
        down_onward, moving, up_got[-1] + [low_in_part], give
    )
    if by_ring:
        input_given.append(given[0])
        moving = [add_round(input_parts, input_given, 3, moving[0])]
        give = [input_parts[chips]]
    up_last, moving, given = last_round(pass_on(up_parts, up_got), moving, down_last, give)
    if by_ring:
        input_given[0] = given[0]
        input_grad = add_round(input_parts, input_given, chips, moving[0])

    low_in_grad = lax.psum_scatter(
        low_in_part, "dp", scatter_dimension=1, tiled=True
    ).astype(F32)
    down_grad = run_sum(down_parts, down_got, down_last)
    up_grad, low_out_grad = run_finish(
        run_sum(up_parts, up_got), up_last, count // (len(starts) * len(groups))
    )
    return (mixed, input_grad, up_grad, down_grad, low_out_grad, low_in_grad)


def solution(mesh):
    return jax.shard_map(
        functools.partial(local, mesh.shape["mp"], mesh.shape["dp"]),
        mesh=mesh,
        in_specs=(
            P(("dp", "mp"), None),
            P(),
            P(),
            P(),
            P("mp", None, None, None),
            P("mp", None),
            P(None, "mp"),
            P("mp", None, None, None),
            P(("dp", "mp"), None),
        ),
        out_specs=(
            P(("dp", "mp"), None),
            P(("dp", "mp"), None),
            P("mp", None, "dp", None),
            P("mp", None, "dp", None),
            P("dp", "mp"),
            P("mp", "dp"),
        ),
        check_vma=False,
    )
```

```python
import functools

import jax
import jax.numpy as jnp
from jax import lax
from jax.experimental import pallas as pl
from jax.experimental.pallas import tpu as pltpu
from jax.sharding import PartitionSpec as P

F32 = jnp.float32
BF16 = jnp.bfloat16
GELU_SCALE = 0.7978845608028654
GELU_CUBE = 0.044715
PER_HIDDEN, PER_PIECES, PER_BACK, PER_GRADIENTS, PER_SPREAD = 4, 6, 4, 4, 6
COST = pl.CostEstimate(flops=1, bytes_accessed=1, transcendentals=0)
VMEM_LIMIT = 60 * 1024 * 1024


def dot_nn(a, b):
    return lax.dot_general(a, b, (((1,), (0,)), ((), ())), preferred_element_type=F32)


def dot_nt(a, b):
    return lax.dot_general(a, b, (((1,), (1,)), ((), ())), preferred_element_type=F32)


def dot_tn(a, b):
    return lax.dot_general(a, b, (((0,), (0,)), ((), ())), preferred_element_type=F32)


def column_block(index, size):
    return pl.ds(pl.multiple_of(index * size, size), size)


def copies_in(chunks, held, sems):
    rows, columns = chunks[0].shape
    blocks = held.shape[0] // rows
    return [
        pltpu.make_async_copy(
            chunk,
            held.at[pl.ds(number % blocks * rows, rows), pl.ds(number // blocks * columns, columns)],
            sems.at[number],
        )
        for number, chunk in enumerate(chunks)
    ]


def fill_zero(total, size):
    @pl.loop(0, total.shape[1] // size)
    def _(block):
        total[:, column_block(block, size)] = jnp.zeros((total.shape[0], size), total.dtype)


def write_out(total, held, outs, sems, size):
    @pl.loop(0, total.shape[1] // size)
    def _(block):
        columns = column_block(block, size)
        held[:, columns] = total[:, columns].astype(held.dtype)

    copies = []
    for number, out in enumerate(outs):
        rows = out.shape[0]
        copies.append(
            pltpu.make_async_copy(held.at[pl.ds(number * rows, rows), :], out, sems.at[number])
        )
    for copy in copies:
        copy.start()
    for copy in copies:
        copy.wait()


def hidden_kernel(chunk_count, wait_count, per, size, up_ref, *refs):
    chunks = refs[:chunk_count]
    low_half, up_weight, low_out = refs[chunk_count : chunk_count + 3]
    hidden, slope, held, in_sems = refs[chunk_count + 3 + wait_count :]
    up_slots = up_weight.shape[1]

    @pl.when(pl.program_id(0) == 0)
    def _():
        copies = copies_in(chunks, held, in_sems)
        for copy in copies:
            copy.start()
        for copy in copies:
            copy.wait()

    for inner in range(per):
        first = (pl.program_id(0) * per + inner) * up_slots
        picked = [held[:, column_block(up_ref[first + slot], size)] for slot in range(up_slots)]
        weights = [up_weight[inner, slot] for slot in range(up_slots)]
        before = dot_nn(
            jnp.concatenate(picked + [low_half[...]], axis=1),
            jnp.concatenate(weights + [low_out[:, inner * size : (inner + 1) * size]], axis=0),
        )
        square = before * before
        bent = jnp.tanh(GELU_SCALE * before * (1.0 + GELU_CUBE * square))
        half = 0.5 * (1.0 + bent)
        hidden[inner] = (before * half).astype(BF16)
        slope[inner] = half + 0.5 * before * (1.0 - bent * bent) * (
            GELU_SCALE * (1.0 + 3.0 * GELU_CUBE * square)
        )


def pieces_kernel(out_count, wait_count, per, size, down_ref, live_ref, *refs):
    hidden, down_weight = refs[:2]
    first_out = 2 + wait_count
    outs = refs[first_out : first_out + out_count]
    held, total, out_sems = refs[first_out + out_count :]
    down_slots = down_weight.shape[1]

    @pl.when(pl.program_id(0) == 0)
    def _():
        fill_zero(total, size)

    for inner in range(per):
        step = pl.program_id(0) * per + inner
        weights = [
            jnp.where(slot < live_ref[step], down_weight[inner, slot], jnp.zeros((), BF16))
            for slot in range(down_slots)
        ]
        pieces = dot_nn(hidden[inner], jnp.concatenate(weights, axis=1))
        for slot in range(down_slots):
            columns = column_block(down_ref[step * down_slots + slot], size)
            total[:, columns] += pieces[:, slot * size : (slot + 1) * size]

    @pl.when(pl.program_id(0) == pl.num_programs(0) - 1)
    def _():
        write_out(total, held, outs, out_sems, size)


def back_kernel(chunk_count, wait_count, per, size, down_ref, live_ref, *refs):
    chunks = refs[:chunk_count]
    slope, down_weight, low_out = refs[chunk_count : chunk_count + 3]
    back_half, back_low, held, sems = refs[chunk_count + 3 + wait_count :]
    down_slots = down_weight.shape[1]

    @pl.when(pl.program_id(0) == 0)
    def _():
        copies = copies_in(chunks, held, sems)
        for copy in copies:
            copy.start()
        back_low[...] = jnp.zeros(back_low.shape, F32)
        for copy in copies:
            copy.wait()

    backs = []
    for inner in range(per):
        step = pl.program_id(0) * per + inner
        wanted = [
            held[:, column_block(down_ref[step * down_slots + slot], size)]
            for slot in range(down_slots)
        ]
        weights = [
            jnp.where(slot < live_ref[step], down_weight[inner, slot], jnp.zeros((), BF16))
            for slot in range(down_slots)
        ]
        back_hidden = dot_nt(jnp.concatenate(wanted, axis=1), jnp.concatenate(weights, axis=1))
        back = (back_hidden * slope[inner]).astype(BF16)
        back_half[inner] = back
        backs.append(back)
    back_low[...] += dot_nt(jnp.concatenate(backs, axis=1), low_out[...])


def load_all(chunks, held, sems):
    @pl.when(pl.program_id(0) == 0)
    def _():
        copies = copies_in(chunks, held, sems)
        for copy in copies:
            copy.start()
        for copy in copies:
            copy.wait()


def write_groups(groups, outs, per, make):
    first = 0
    for number, (length, way) in enumerate(groups):
        steps = length // per
        inside = (pl.program_id(0) >= first) & (pl.program_id(0) < first + steps)

        @pl.when(inside)
        def _(number=number, way=way):
            own, send, passed = outs[3 * number : 3 * number + 3]
            for inner in range(per):
                for slot in range(own.shape[1]):
                    own[inner, slot] = make(inner, slot, 0)
                    passed[inner, slot] = make(inner, slot, 3 - way).astype(BF16)
                    send[0, inner, slot] = make(inner, slot, way).astype(BF16)
                    send[1, inner, slot] = make(inner, slot, 3).astype(BF16)

        first += steps


def down_kernel(
    chunk_count, wait_count, first_step, per, groups, size, down_ref, live_ref, quarter_ref, *refs
):
    chunks = refs[:chunk_count]
    hidden = refs[chunk_count]
    outs = refs[chunk_count + 1 + wait_count : -3]
    held, part, sems = refs[-3:]
    slots, rows = outs[0].shape[1:3]
    load_all(chunks, held, sems)
    step = first_step + pl.program_id(0) * per
    for inner in range(per):
        wanted = [
            held[:, column_block(down_ref[(step + inner) * slots + slot], size)]
            for slot in range(slots)
        ]
        part[inner] = dot_tn(hidden[inner], jnp.concatenate(wanted, axis=1))

    def make(inner, slot, which):
        keep = (slot < live_ref[step + inner]).astype(F32)
        first = pl.multiple_of(quarter_ref[which] * rows, rows)
        return part[inner, pl.ds(first, rows), slot * size : (slot + 1) * size] * keep

    write_groups(groups, outs, per, make)


def up_kernel(chunk_count, wait_count, first_step, per, groups, size, up_ref, quarter_ref, *refs):
    chunks = refs[:chunk_count]
    low_half, back_half = refs[chunk_count : chunk_count + 2]
    outs = refs[chunk_count + 2 + wait_count : -3]
    held, part, sems = refs[-3:]
    slots, rows = outs[0].shape[1] - 1, outs[0].shape[2]
    load_all(chunks, held, sems)
    step = first_step + pl.program_id(0) * per
    for inner in range(per):
        picked = [
            held[:, column_block(up_ref[(step + inner) * slots + slot], size)]
            for slot in range(slots)
        ]
        part[inner] = dot_tn(jnp.concatenate(picked + [low_half[...]], axis=1), back_half[inner])

    def make(inner, slot, which):
        first = pl.multiple_of(quarter_ref[which] * rows + slot * size, rows)
        return part[inner, pl.ds(first, rows), :]

    write_groups(groups, outs, per, make)


def spread_kernel(out_count, wait_count, per, size, up_ref, rank_ref, *refs):
    back_half, up_weight, back_low, low_in = refs[:4]
    first_out = 4 + wait_count
    outs = refs[first_out : first_out + out_count]
    held, total, out_sems = refs[first_out + out_count :]
    up_slots = up_weight.shape[1]

    @pl.when(pl.program_id(0) == 0)
    def _():
        fill_zero(total, size)
        first = rank_ref[0] * (low_in.shape[0] // size)

        @pl.loop(0, low_in.shape[0] // size)
        def _(block):
            rows = pl.ds(pl.multiple_of(block * size, size), size)
            side = dot_nt(back_low[...], low_in[rows, :])
            total[:, column_block(first + block, size)] = side

    for inner in range(per):
        step = pl.program_id(0) * per + inner
        weights = jnp.concatenate([up_weight[inner, slot] for slot in range(up_slots)], axis=0)
        spread = dot_nt(back_half[inner], weights)
        for slot in range(up_slots):
            columns = column_block(up_ref[step * up_slots + slot], size)
            total[:, columns] += spread[:, slot * size : (slot + 1) * size]

    @pl.when(pl.program_id(0) == pl.num_programs(0) - 1)
    def _():
        write_out(total, held, outs, out_sems, size)


def whole_spec(array):
    zeros = (0,) * array.ndim
    return pl.BlockSpec(array.shape, lambda i, *_: zeros)


def any_spec():
    return pl.BlockSpec(memory_space=pl.ANY)


def block_spec(array, per, first=0):
    rest = (0,) * (array.ndim - 1)
    return pl.BlockSpec((per,) + array.shape[1:], lambda i, *_: (i + first // per,) + rest)


def blocks_per_step(count, most):
    return max(per for per in range(1, most + 1) if count % per == 0)


def params():
    return pltpu.CompilerParams(
        dimension_semantics=("arbitrary",), vmem_limit_bytes=VMEM_LIMIT
    )


def shape(dims, dtype):
    return jax.ShapeDtypeStruct(dims, dtype)


def run_hidden(scalars, chunks, low_half, up_weight, low_out, waits, size):
    count, tok_total, width = up_weight.shape[0], low_half.shape[0], chunks[0].shape[1]
    per = blocks_per_step(count, PER_HIDDEN)
    hidden = shape((count, tok_total, size), BF16)
    slope = shape((count, tok_total, size), F32)
    return pl.pallas_call(
        functools.partial(hidden_kernel, len(chunks), len(waits), per, size),
        out_shape=[hidden, slope],
        grid_spec=pltpu.PrefetchScalarGridSpec(
            num_scalar_prefetch=len(scalars),
            grid=(count // per,),
            in_specs=[any_spec()] * len(chunks)
            + [
                whole_spec(low_half),
                block_spec(up_weight, per),
                pl.BlockSpec((low_out.shape[0], per * size), lambda i, *_: (0, i)),
            ]
            + [any_spec()] * len(waits),
            out_specs=[block_spec(hidden, per), block_spec(slope, per)],
            scratch_shapes=[
                pltpu.VMEM((tok_total, width), BF16),
                pltpu.SemaphoreType.DMA((len(chunks),)),
            ],
        ),
        compiler_params=params(),
        cost_estimate=COST,
        name="hidden",
    )(*scalars, *chunks, low_half, up_weight, low_out, *waits)


def run_pieces(scalars, hidden, down_weight, waits, out_shapes, width, size):
    count, tok_total = hidden.shape[:2]
    per = blocks_per_step(count, PER_PIECES)
    return pl.pallas_call(
        functools.partial(pieces_kernel, len(out_shapes), len(waits), per, size),
        out_shape=[shape(dims, BF16) for dims in out_shapes],
        grid_spec=pltpu.PrefetchScalarGridSpec(
            num_scalar_prefetch=len(scalars),
            grid=(count // per,),
            in_specs=[block_spec(hidden, per), block_spec(down_weight, per)] + [any_spec()] * len(waits),
            out_specs=[any_spec()] * len(out_shapes),
            scratch_shapes=[
                pltpu.VMEM((tok_total, width), BF16),
                pltpu.VMEM((tok_total, width), F32),
                pltpu.SemaphoreType.DMA((len(out_shapes),)),
            ],
        ),
        compiler_params=params(),
        cost_estimate=COST,
        name="pieces",
    )(*scalars, hidden, down_weight, *waits)


def run_back(scalars, chunks, slope, down_weight, low_out, waits, width, size):
    count, tok_total = slope.shape[:2]
    per = blocks_per_step(count, PER_BACK)
    back_half = shape((count, tok_total, size), BF16)
    back_low = shape((tok_total, low_out.shape[0]), F32)
    return pl.pallas_call(
        functools.partial(back_kernel, len(chunks), len(waits), per, size),
        out_shape=[back_half, back_low],
        grid_spec=pltpu.PrefetchScalarGridSpec(
            num_scalar_prefetch=len(scalars),
            grid=(count // per,),
            in_specs=[any_spec()] * len(chunks)
            + [
                block_spec(slope, per),
                block_spec(down_weight, per),
                pl.BlockSpec((low_out.shape[0], per * size), lambda i, *_: (0, i)),
            ]
            + [any_spec()] * len(waits),
            out_specs=[block_spec(back_half, per), whole_spec(back_low)],
            scratch_shapes=[
                pltpu.VMEM((tok_total, width), BF16),
                pltpu.SemaphoreType.DMA((len(chunks),)),
            ],
        ),
        compiler_params=params(),
        cost_estimate=COST,
        name="back",
    )(*scalars, *chunks, slope, down_weight, low_out, *waits)


def run_gradients(
    kernel, scalars, chunks, whole, blocks, waits, first, groups, slots, part_shape, parts, width
):
    per = min(blocks_per_step(length, PER_GRADIENTS) for length, _ in groups)
    tok_total, size = blocks.shape[1:]
    rows = size // parts
    outs, specs, step = [], [], 0
    for length, _ in groups:
        last = length // per - 1

        def place(i, start=step, last=last):
            return jnp.clip(i - start, 0, last)

        outs += [
            shape((length, slots, rows, size), F32),
            shape((2, length, slots, rows, size), BF16),
            shape((length, slots, rows, size), BF16),
        ]
        one = pl.BlockSpec((per, slots, rows, size), lambda i, *_, at=place: (at(i), 0, 0, 0))
        two = pl.BlockSpec((2, per, slots, rows, size), lambda i, *_, at=place: (0, at(i), 0, 0, 0))
        specs += [one, two, one]
        step += length // per
    results = pl.pallas_call(
        functools.partial(kernel, len(chunks), len(waits), first, per, groups, size),
        out_shape=outs,
        grid_spec=pltpu.PrefetchScalarGridSpec(
            num_scalar_prefetch=len(scalars),
            grid=(step,),
            in_specs=[any_spec()] * len(chunks)
            + [whole_spec(array) for array in whole]
            + [block_spec(blocks, per, first)]
            + [any_spec()] * len(waits),
            out_specs=specs,
            scratch_shapes=[
                pltpu.VMEM((tok_total, width), BF16),
                pltpu.VMEM((per,) + part_shape, F32),
                pltpu.SemaphoreType.DMA((len(chunks),)),
            ],
        ),
        compiler_params=params(),
        cost_estimate=COST,
        name=kernel.__name__,
    )(*scalars, *chunks, *whole, blocks, *waits)
    return [results[3 * number : 3 * number + 3] for number in range(len(groups))]


def run_spread(scalars, back_half, up_weight, back_low, low_in, waits, out_shapes, width, size):
    count, tok_total = back_half.shape[:2]
    per = blocks_per_step(count, PER_SPREAD)
    return pl.pallas_call(
        functools.partial(spread_kernel, len(out_shapes), len(waits), per, size),
        out_shape=[shape(dims, BF16) for dims in out_shapes],
        grid_spec=pltpu.PrefetchScalarGridSpec(
            num_scalar_prefetch=len(scalars),
            grid=(count // per,),
            in_specs=[
                block_spec(back_half, per),
                block_spec(up_weight, per),
                whole_spec(back_low),
                whole_spec(low_in),
            ]
            + [any_spec()] * len(waits),
            out_specs=[any_spec()] * len(out_shapes),
            scratch_shapes=[
                pltpu.VMEM((tok_total, width), BF16),
                pltpu.VMEM((tok_total, width), F32),
                pltpu.SemaphoreType.DMA((len(out_shapes),)),
            ],
        ),
        compiler_params=params(),
        cost_estimate=COST,
        name="spread",
    )(*scalars, back_half, up_weight, back_low, low_in, *waits)


def pass_kernel(half_count, *refs):
    out, first = refs[-1], 0
    for half in range(half_count):
        passed, got = refs[2 * half : 2 * half + 2]
        length = passed.shape[0]
        out[first : first + length] = (passed[...].astype(F32) + got[0].astype(F32)).astype(BF16)
        first += length


def run_pass(halves):
    length = sum(passed.shape[0] for passed, _ in halves)
    out = shape((length,) + halves[0][0].shape[1:], BF16)
    specs = []
    for passed, got in halves:
        specs += [
            whole_spec(passed),
            pl.BlockSpec((1,) + got.shape[1:], lambda i: (1, 0, 0, 0, 0)),
        ]
    return pl.pallas_call(
        functools.partial(pass_kernel, len(halves)),
        out_shape=out,
        grid=(1,),
        in_specs=specs,
        out_specs=whole_spec(out),
        compiler_params=params(),
        cost_estimate=COST,
        name="pass_on",
    )(*[array for pair in halves for array in pair])


def add_kernel(*refs):
    total = refs[0][...].astype(F32)
    for part in refs[1:-1]:
        total = total + part[...].astype(F32)
    refs[-1][...] = total.astype(BF16)


def run_add(arrays):
    rows, width = arrays[0].shape
    steps = 2 if width % 256 == 0 else 1
    spec = pl.BlockSpec((rows, width // steps), lambda i: (0, i))
    return pl.pallas_call(
        add_kernel,
        out_shape=shape((rows, width), BF16),
        grid=(steps,),
        in_specs=[spec] * len(arrays),
        out_specs=spec,
        compiler_params=params(),
        cost_estimate=COST,
        name="add_rows",
    )(*arrays)


def low_kernel(chunk_count, place_ref, *refs):
    chunks, out = refs[: 2 * chunk_count], refs[-1]
    weight, other_weight = refs[2 * chunk_count : 2 * chunk_count + 2]
    own = jnp.concatenate([chunk[...] for chunk in chunks[:chunk_count]], axis=0)
    other = jnp.concatenate([chunk[...] for chunk in chunks[chunk_count:]], axis=0)
    out[...] = dot_nn(own, weight[...]) + dot_nn(other, other_weight[...])


def run_low(places, chunks, weight, other_weight, waits):
    rows, columns = chunks[0].shape[0], weight.shape[0]
    out = shape((len(chunks) * rows, weight.shape[1]), F32)
    return pl.pallas_call(
        functools.partial(low_kernel, len(chunks)),
        out_shape=out,
        grid_spec=pltpu.PrefetchScalarGridSpec(
            num_scalar_prefetch=1,
            grid=(1,),
            in_specs=[pl.BlockSpec((rows, columns), lambda i, at: (0, at[0]))] * len(chunks)
            + [pl.BlockSpec((rows, columns), lambda i, at: (0, at[1]))] * len(chunks)
            + [whole_spec(weight), whole_spec(other_weight)]
            + [any_spec()] * len(waits),
            out_specs=whole_spec(out),
        ),
        compiler_params=params(),
        cost_estimate=COST,
        name="low_part",
    )(places, *chunks, *chunks, weight, other_weight, *waits)


def side_kernel(place_ref, *refs):
    back_low, out = refs[-2:]
    columns = jnp.concatenate([chunk[...] for chunk in refs[:-2]], axis=0)
    out[...] = dot_tn(columns, back_low[...]).astype(BF16)


def run_side(places, chunks, back_low, col_width):
    rows = chunks[0].shape[0]
    out = shape((col_width, back_low.shape[1]), BF16)
    return pl.pallas_call(
        side_kernel,
        out_shape=out,
        grid_spec=pltpu.PrefetchScalarGridSpec(
            num_scalar_prefetch=1,
            grid=(1,),
            in_specs=[pl.BlockSpec((rows, col_width), lambda i, at: (0, at[0]))] * len(chunks)
            + [whole_spec(back_low)],
            out_specs=whole_spec(out),
        ),
        compiler_params=params(),
        cost_estimate=COST,
        name="low_in_part",
    )(places, *chunks, back_low)


def sum_kernel(places, own_count, *refs):
    out, first = refs[-1], 0
    for number, (last, start) in enumerate(places):
        own, got = refs[2 * number : 2 * number + 2]
        length = own.shape[0]
        total = own[...] + got[0].astype(F32)
        if last is not None:
            total = total + refs[2 * own_count + last][start : start + length].astype(F32)
        out[first : first + length] = total
        first += length


def run_sum(parts, gots, lasts=()):
    pairs, firsts = [], [0] * len(parts[0])
    for part, gots_here in zip(parts, gots):
        for number, (own, got) in enumerate(zip(part, gots_here)):
            pairs.append((own[0], got, number, firsts[number]))
            firsts[number] += own[0].shape[0]
    places = [(number, start) if lasts else (None, 0) for _, _, number, start in pairs]
    specs, arrays = [], []
    for own, got, _, _ in pairs:
        specs += [
            whole_spec(own),
            pl.BlockSpec((1,) + got.shape[1:], lambda i: (0, 0, 0, 0, 0)),
        ]
        arrays += [own, got]
    specs += [whole_spec(last) for last in lasts]
    length = sum(own.shape[0] for own, _, _, _ in pairs)
    out = shape((length,) + pairs[0][0].shape[1:], F32)
    return pl.pallas_call(
        functools.partial(sum_kernel, places, len(pairs)),
        out_shape=out,
        grid=(1,),
        in_specs=specs,
        out_specs=whole_spec(out),
        compiler_params=params(),
        cost_estimate=COST,
        name="sums",
    )(*arrays, *lasts)


def finish_kernel(group_count, *refs):
    before = refs[0]
    lasts = refs[1 : 1 + group_count]
    blocks, side = refs[1 + group_count :]
    size = blocks.shape[3]
    for number, last in enumerate(lasts):

        @pl.when(pl.program_id(0) % group_count == number)
        def _(last=last):
            for block in range(blocks.shape[0]):
                total = before[block] + last[block].astype(F32)
                blocks[block] = total[:-1]
                side[:, block * size : (block + 1) * size] = total[-1]


def run_finish(before, lasts, group):
    count, slots, rows, size = before.shape
    part = (group, slots, rows, size)
    return pl.pallas_call(
        functools.partial(finish_kernel, len(lasts)),
        out_shape=[shape((count, slots - 1, rows, size), F32), shape((rows, count * size), F32)],
        grid=(count // group,),
        in_specs=[pl.BlockSpec(part, lambda i: (i, 0, 0, 0))]
        + [pl.BlockSpec(part, lambda i: (i // len(lasts), 0, 0, 0))] * len(lasts),
        out_specs=[
            pl.BlockSpec((group, slots - 1, rows, size), lambda i: (i, 0, 0, 0)),
            pl.BlockSpec((rows, group * size), lambda i: (0, i)),
        ],
        compiler_params=params(),
        cost_estimate=COST,
        name="finish",
    )(before, *lasts)


def fence(values, waits):
    values, waits = list(values), list(waits)
    return list(pl.pallas_call(
        lambda *refs: None,
        out_shape=[shape(value.shape, value.dtype) for value in values],
        in_specs=[any_spec()] * (len(values) + len(waits)),
        out_specs=[any_spec()] * len(values),
        input_output_aliases={number: number for number in range(len(values))},
        compiler_params=pltpu.CompilerParams(vmem_limit_bytes=VMEM_LIMIT),
        cost_estimate=COST,
        name="fence",
    )(*values, *waits))


def local(mp_size, dp_size, tokens, up_blocks, down_blocks, down_live, up_weight, low_in, low_out, down_weight, cotangent):
    count, up_slots, size = up_weight.shape[:3]
    rows, width = tokens.shape
    tok_total = rows * mp_size
    col_width = low_in.shape[0]
    rank = lax.axis_index("mp")
    part = lax.axis_index("dp")
    chips = mp_size // 2
    by_ring = rows % 16 == 0 and chips == 4
    swap = [(i, i ^ 1) for i in range(mp_size)]
    step_x = [(i, i ^ 1) for i in range(dp_size)]
    step_y = [(i, i ^ 2) for i in range(dp_size)]

    up_index = lax.dynamic_slice_in_dim(up_blocks, rank * count, count, 0).reshape(-1)
    down_index = lax.dynamic_slice_in_dim(down_blocks, rank * count, count, 0).reshape(-1)
    live = lax.dynamic_slice_in_dim(down_live, rank * count, count, 0)
    quarters = part ^ jnp.arange(dp_size, dtype=jnp.int32)
    out_shapes = [(rows, width)] * mp_size if by_ring else [(tok_total, width)]

    def swapped(piece):
        return lax.ppermute(piece, "mp", swap)

    def shifted(piece, by):
        return lax.ppermute(piece, "mp", [(i, (i + 2 * by) % mp_size) for i in range(mp_size)])

    def add_round(parts, given, place, *moved):
        return run_add([parts[place % chips], given[place % chips], *moved])

    def scatter_whole(parts):
        whole = parts[0].reshape(mp_size, rows, width)
        return lax.psum_scatter(whole, "mp", scatter_dimension=0)

    def over_dp(value, way):
        return lax.ppermute(value, "dp", step_y if way == 2 else step_x)

    def pass_on(parts, gots):
        return [
            run_pass([(part[n][2], got[n]) for part, got in zip(parts, gots)])
            for n in range(len(groups))
        ]

    def all_rows(total):
        same = total.astype(BF16)
        other, early = swapped(same), (chips - 1) * rows
        pieces = in_rows([same[:early], same[early:]], [other[:early], other[early:]])
        return same, jnp.concatenate(pieces, 0)

    def sum_rows(chip_sum):
        sent = chip_sum.astype(BF16)
        total = chip_sum
        for by in range(1, chips):
            got = shifted(sent, by)
            total = total + jnp.roll(got, by * rows, axis=0).astype(F32)
        return all_rows(total)

    def sum_rows_in_pairs(chip_sum, waits):
        near = [(i, i ^ 2) for i in range(mp_size)]
        far = [(i, i ^ 4) for i in range(mp_size)]
        got = fence([lax.ppermute(chip_sum.astype(BF16), "mp", near)], waits)[0].astype(F32)
        even = (rank // 2) % 2 == 0
        got = jnp.where(even, jnp.roll(got, -rows, axis=0), jnp.roll(got, rows, axis=0))
        pair_sum = chip_sum + got
        got = lax.ppermute(pair_sum.astype(BF16), "mp", far).astype(F32)
        return all_rows(pair_sum + jnp.roll(got, 2 * rows, axis=0))

    def sum_whole(partial):
        low = lax.psum_scatter(partial, "mp", scatter_dimension=0, tiled=True).astype(BF16)
        return lax.all_gather(low, "mp", axis=0, tiled=True)

    def in_rows(same, other):
        return same[:-1] + other[:-1] + same[-1:] + other[-1:]

    def by_core(parts):
        early = chips - 1
        return parts[:early] + parts[-2:-1] + parts[early:-2] + parts[-1:]

    def take_columns(piece, place):
        return lax.dynamic_slice_in_dim(piece, place * col_width, col_width, 1)

    if by_ring:
        places = jnp.stack([rank, rank ^ 1]).astype(jnp.int32)
        other_low = swapped(low_in)
        x_same, x_other = [tokens], []
        y_same, y_other = [cotangent], [swapped(cotangent)]
        for step in range(chips):
            if step < chips - 1:
                if step == 2:
                    x_same[2] = fence(x_same[2:], x_other + y_other + [other_low])[0]
                x_same.append(shifted(x_same[step], 1))
                x_other.append(swapped(x_same[step]))
        x_other.append(swapped(x_same[-1]))
        x_chunks = in_rows(x_same, x_other)
        low_same, low_half = sum_rows(
            run_low(places, x_same, low_in, other_low, x_other[2:3])
        )
        arriving = shifted(cotangent, 1)
        arrived = fence([arriving], [low_same])[0]
        y_same.append(arrived)
        y_other.append(swapped(arrived))
        arriving = shifted(arrived, 1)
    else:
        x_chunks = [lax.all_gather(tokens, "mp", axis=0, tiled=True)]
        y_chunks = [lax.all_gather(cotangent, "mp", axis=0, tiled=True)]
        low = jnp.dot(take_columns(x_chunks[0], rank), low_in, preferred_element_type=F32)
        low_half = sum_whole(low)
    hidden, slope = run_hidden((up_index,), x_chunks, low_half, up_weight, low_out, [], size)
    if by_ring:
        arrived, hidden = fence([arriving, hidden], y_other + [slope])
        y_same.append(arrived)
        y_other.append(swapped(arrived))
        arriving = shifted(arrived, 1)
    mixed_parts = list(
        run_pieces((down_index, live), hidden, down_weight, [], out_shapes, width, size)
    )
    if by_ring:
        mixed_parts = by_core(mixed_parts)
        arrived, *mixed_parts = fence([arriving] + mixed_parts, y_other)
        y_same.append(arrived)
        y_other.append(swapped(arrived))
        y_chunks = in_rows(y_same, y_other)
        mixed_given = [None] + [swapped(piece) for piece in mixed_parts[chips + 1 :]]

    down_slots = down_weight.shape[1]
    if count % 12 == 0:
        groups, starts = ((count // 4, 2), (count // 4, 1)), (0, count // 2)
        down_groups = ((count // 6, 2), (count // 6, 1), (count // 3, 2), (count // 3, 1))
    else:
        groups, starts = ((count, 2),), (0,)
        down_groups = groups

    def up_part(start, waits):
        return run_gradients(
            up_kernel, (up_index, quarters), x_chunks, [low_half], back_half, waits, start, groups,
            up_slots + 1, ((up_slots + 1) * size, size), dp_size, width,
        )

    def send_round(parts, moving, waits, give=()):
        here = [part[1] for part in parts]
        sent = fence(here + list(give), waits + moving)
        got = [over_dp(value, way) for value, (_, way) in zip(sent, groups)]
        moved = [shifted(value, 1) for value in moving]
        return sent[0], got, moved, [swapped(value) for value in sent[len(here) :]]

    down_all = run_gradients(
        down_kernel, (down_index, live, quarters), y_chunks, [], hidden, [], 0, down_groups,
        down_slots, (size, down_slots * size), dp_size, width,
    )
    down_parts = [down_all[n : n + len(groups)] for n in range(0, len(down_all), len(groups))]
    waits = [y_other[-1]] + mixed_given[1:] if by_ring else []
    token, got, _, _ = send_round(down_parts[0], [], waits)
    down_got, moving = [got], []
    if by_ring:
        moved = shifted(add_round(mixed_parts, mixed_given, 1), 1)
        moving = [add_round(mixed_parts, mixed_given, 2, moved)]
    back_half, back_low = run_back(
        (down_index, live), y_chunks, slope, down_weight, low_out, [token], width, size
    )
    if len(down_parts) > 1:
        here = [part[1] for part in down_parts[1]]
        token, *sent = fence([back_low] + here, down_got[0] + moving)
        back_low = token
        down_got.append([over_dp(value, way) for value, (_, way) in zip(sent, groups)])
    up_parts = [up_part(starts[0], [token])]
    waits = [up_parts[0][0][0]]
    if by_ring:
        low = by_core([back_low[n * rows : (n + 1) * rows] for n in range(mp_size)])
        chip_sum = jnp.concatenate(low[:chips], 0) + swapped(jnp.concatenate(low[chips:], 0))
        _, back_low = sum_rows_in_pairs(chip_sum, waits)
        moving = [add_round(mixed_parts, mixed_given, 3, shifted(moving[0], 1))]
    else:
        back_low = sum_whole(back_low)
    give = [mixed_parts[chips]] if by_ring else []
    token, got, moving, given = send_round(
        up_parts[0], moving, down_got[-1] + waits + [back_low], give
    )
    up_got = [got]
    if len(starts) > 1:
        up_parts.append(up_part(starts[1], [token]))
    if by_ring:
        mixed_given[0] = given[0]
    input_parts = list(
        run_spread(
            (up_index, rank.reshape(1)),
            back_half, up_weight, back_low, low_in, [token], out_shapes, width, size,
        )
    )
    if by_ring:
        low_in_part = run_side(places, x_chunks, back_low, col_width)
    else:
        low_in_part = lax.dot_general(
            take_columns(x_chunks[0], rank), back_low, (((0,), (0,)), ((), ())),
            preferred_element_type=F32,
        ).astype(BF16)
    down_onward = pass_on(down_parts, down_got)
    waits, give = up_got[0], []
    if by_ring:
        input_parts = by_core(input_parts)
        mixed = add_round(mixed_parts, mixed_given, chips, moving[0])
        waits, give = waits + moving, input_parts[chips + 1 : chips + 3]
    else:
        mixed, input_grad = scatter_whole(mixed_parts), scatter_whole(input_parts)
    if len(starts) > 1:
        token, got, _, given = send_round(up_parts[1], [], waits, give)
        up_got.append(got)
    if by_ring:
        input_given = [None] + given
        moving = [shifted(add_round(input_parts, input_given, 1), 1)]
        moving = [add_round(input_parts, input_given, 2, moving[0])]

    def last_round(onward, moving, waits, give=()):
        sent = fence(onward + list(give), waits + moving)
        last = [over_dp(value, 3 - way) for value, (_, way) in zip(sent, groups)]
        moved = [shifted(value, 1) for value in moving]
        return last, moved, [swapped(value) for value in sent[len(groups) :]]

    give = [input_parts[chips + 3]] if by_ring else []
    down_last, moving, given = last_round(
        down_onward, moving, up_got[-1] + [low_in_part, mixed], give
    )
    if by_ring:
        input_given.append(given[0])
        moving = [add_round(input_parts, input_given, 3, moving[0])]
        give = [input_parts[chips]]
    up_last, moving, given = last_round(pass_on(up_parts, up_got), moving, down_last, give)
    if by_ring:
        input_given[0] = given[0]
        input_grad = add_round(input_parts, input_given, chips, moving[0])

    low_in_grad = lax.psum_scatter(
        low_in_part, "dp", scatter_dimension=1, tiled=True
    ).astype(F32)
    down_grad = run_sum(down_parts, down_got, down_last)
    up_grad, low_out_grad = run_finish(
        run_sum(up_parts, up_got), up_last, count // (len(starts) * len(groups))
    )
    return (mixed, input_grad, up_grad, down_grad, low_out_grad, low_in_grad)


def solution(mesh):
    return jax.shard_map(
        functools.partial(local, mesh.shape["mp"], mesh.shape["dp"]),
        mesh=mesh,
        in_specs=(
            P(("dp", "mp"), None),
            P(),
            P(),
            P(),
            P("mp", None, None, None),
            P("mp", None),
            P(None, "mp"),
            P("mp", None, None, None),
            P(("dp", "mp"), None),
        ),
        out_specs=(
            P(("dp", "mp"), None),
            P(("dp", "mp"), None),
            P("mp", None, "dp", None),
            P("mp", None, "dp", None),
            P("dp", "mp"),
            P("mp", "dp"),
        ),
        check_vma=False,
    )
```
